32 devices in a mesh: op: 4 (over x, core), sec: 8 (over z, y).
Axes of the slice: x: 2, y: 2, z: 4, core: 2. Of those that a mesh axis runs over, the one named last changes fastest.
Arguments:
- wavefunction: bfloat16 [2048, 3, 1024], P('sec'), may hold values from -6 to 6
- left_ops: bfloat16 [2048, 12, 256], P('sec', 'op'), may hold values from -0.375 to 0.375
- right_ops: bfloat16 [12, 8, 128, 128], P('op', 'sec'), may hold values from -0.15625 to 0.15625
- term_shift: int32 [12], P('op'), may hold values from -1 to 1
Outputs:
- applied: bfloat16 [2048, 3, 1024], P('sec', None, 'op')
The draws below stay inside these ranges and needn't reach their ends.
All inputs are finite; a program needn't handle non-finite values.
Results may differ from the reference program's by a relative error of at most 0.017.
Values may be sent and summed in bfloat16 or wider, within the bound.
No kernel may reach another device: no remote copies, remote signals or barrier semaphores. Data moves between devices by JAX's collectives and lax.ppermute only.
A program may use at most 128 MiB of HBM per device.

```python
import jax
import jax.numpy as jnp
from jax import lax

ML = 256
MR = 128
VECS = 3
K_DEV = 3
KTERMS = 12
LSECT = 8
RSECT = 8
NL = 2048
NR = 1024
N_OP = 4


def touch_ends(drawn, stream_key, smallest, largest):
    extent = drawn.shape
    place = [jax.random.randint(jax.random.fold_in(stream_key, axis), (), 0, extent[axis]) for axis in range(len(extent))]
    drawn = drawn.at[tuple(place)].set(smallest)
    longest = extent.index(max(extent))
    place[longest] = (place[longest] + 1) % extent[longest]
    return drawn.at[tuple(place)].set(largest)


def levels(stream_key, extent, split, smallest, largest):
    def one(dim, parts):
        steps = jax.random.uniform(jax.random.fold_in(jax.random.fold_in(stream_key, 6), dim), (parts,), jnp.float32, smallest / len(split), largest / len(split))
        return jnp.repeat(jnp.exp(steps), extent[dim] // parts).reshape((-1,) + (1,) * (len(extent) - dim - 1))

    gain = one(*split[0])
    for cut in split[1:]:
        gain = gain * one(*cut)
    return gain


def bell_draw(rng, dims, width, limit, cuts=(), held_as=jnp.bfloat16):
    values = width * jax.random.normal(rng, dims, jnp.float32)
    if cuts:
        values = values * levels(rng, dims, cuts, -0.22, 0.18)
    return jnp.clip(values, -limit, limit).astype(held_as)


def setup_inputs(seed: int = 0) -> dict:
    keys = jax.random.split(jax.random.key(seed), 5)
    return {
        "wavefunction": bell_draw(keys[0], (NL, VECS, NR), 1.0, 6.0, ((0, 8),)),
        "left_ops": bell_draw(keys[1], (NL, KTERMS, ML), ML ** -0.5, 0.375, ((0, 8), (1, 4))),
        "right_ops": bell_draw(keys[2], (KTERMS, RSECT, MR, MR), (MR * KTERMS) ** -0.5, 0.15625, ((0, 4), (1, 8))),
        "term_shift": touch_ends(jax.random.randint(keys[3], (KTERMS,), -1, 2), jax.random.fold_in(keys[3], 1), -1, 1).astype(jnp.int32),
    }


def reference(wavefunction, left_ops, right_ops, term_shift):
    blocks = wavefunction.astype(jnp.float32).reshape(LSECT, ML, VECS, NR)
    left_all = left_ops.astype(jnp.float32).reshape(LSECT, ML, KTERMS, ML)
    right_all = right_ops.astype(jnp.float32)
    sector_rows = jnp.arange(LSECT)
    sector_cols = jnp.arange(RSECT)
    applied = jnp.zeros((NL, VECS, NR), jnp.float32)
    for group in range(N_OP):
        partial_sum = jnp.zeros((NL, VECS, NR), jnp.float32)
        for inner in range(K_DEV):
            term = group * K_DEV + inner
            offset = term_shift[term]
            source = jnp.einsum("aij,ajvn->aivn", left_all[:, :, term, :], blocks).astype(jnp.bfloat16)
            source = lax.optimization_barrier(source)
            placed = jnp.roll(source, offset, axis=0)
            row_valid = (sector_rows - offset >= 0) & (sector_rows - offset < LSECT)
            placed = jnp.where(row_valid[:, None, None, None], placed, jnp.zeros((), jnp.bfloat16))
            columns = jnp.roll(placed.reshape(NL, VECS, RSECT, MR), -offset, axis=2)
            col_valid = (sector_cols + offset >= 0) & (sector_cols + offset < RSECT)
            result = jnp.einsum("nvbk,bkm->nvbm", columns.astype(jnp.float32), right_all[term])
            result = jnp.where(col_valid[None, None, :, None], result, jnp.zeros((), jnp.float32))
            partial_sum = partial_sum + result.reshape(NL, VECS, NR)
        rounded = lax.optimization_barrier(partial_sum.astype(jnp.bfloat16))
        applied = applied + rounded.astype(jnp.float32)
    return applied.astype(jnp.bfloat16)
```

```python
import functools

import jax
import jax.numpy as jnp
from jax import lax
from jax.experimental import pallas as pl
from jax.experimental.pallas import tpu as pltpu
from jax.sharding import PartitionSpec as P

ML = 256
MR = 128
VECS = 3
VMEM_BYTES = 48 * 1024 * 1024


def over_op(x, n_op, bit):
    return lax.ppermute(x, "op", [(o, o ^ bit) for o in range(n_op)])


def over_sec(x, n_sec, bit):
    return lax.ppermute(x, "sec", [(d, d ^ bit) for d in range(n_sec)])


def doubled(piece, n_op):
    pieces = [piece]
    bit = n_op // 2
    while bit:
        pieces = pieces + [over_op(p, n_op, bit) for p in pieces]
        bit //= 2
    return pieces


def shifts_of(term_shift, n_op):
    held = term_shift[None]
    bit = n_op // 2
    while bit:
        held = jnp.concatenate([held, over_op(held, n_op, bit)])
        bit //= 2
    return held


def right_classes(right_ops, n_op, n_sec):
    per = n_sec // n_op
    op, sec = lax.axis_index("op"), lax.axis_index("sec")
    held = right_ops.reshape((1,) + right_ops.shape[:1] + right_ops.shape[2:])
    bit = n_op // 2
    while bit > 1:
        same = (op & bit) == ((sec // per) & bit)
        first, second = [], []
        for o in range(n_op):
            for d in range(n_sec):
                source = o * n_sec + d
                if (o & bit) == ((d // per) & bit):
                    first.append((source, o * n_sec + (d ^ (bit * per))))
                else:
                    first.append((source, (o ^ bit) * n_sec + d))
                    second.append((source, (o ^ bit) * n_sec + (d ^ (bit * per))))
        one = lax.ppermute(held, ("op", "sec"), first)
        two = lax.ppermute(held, ("op", "sec"), second)
        held = jnp.concatenate([jnp.where(same, held, one), jnp.where(same, one, two)])
        bit //= 2
    classes = [held]
    bit = 1
    while bit < per:
        classes = classes + [over_sec(c, n_sec, bit) for c in classes]
        bit *= 2
    same = (op & 1) == ((sec // per) & 1)
    done = []
    for own in classes:
        other = over_sec(own, n_sec, per)
        mine, theirs = jnp.where(same, own, other), jnp.where(same, other, own)
        done.append([mine, over_op(theirs, n_op, 1)])
    return done


def left_kernel(n_op, place, shift, *refs):
    *lefts, wave, z_ref, window, sems = refs
    width = z_ref.shape[3]
    per = width // MR
    terms = lefts[0].shape[0]
    op = place[0]
    start = pl.multiple_of(op * width, MR)
    middle = pltpu.make_async_copy(
        wave.at[:, :, pl.ds(start, width)], window.at[:, :, pl.ds(MR, width)], sems.at[0]
    )
    middle.start()

    def edge(valid, source, target, sem):
        @pl.when(valid)
        def _():
            copy = pltpu.make_async_copy(
                wave.at[:, :, pl.ds(pl.multiple_of(source, MR), MR)], window.at[:, :, pl.ds(target, MR)], sem
            )
            copy.start()
            copy.wait()

        @pl.when(jnp.logical_not(valid))
        def _():
            window[:, :, pl.ds(target, MR)] = jnp.zeros((VECS, ML, MR), jnp.bfloat16)

    edge(op > 0, start - MR, 0, sems.at[1])
    edge(op < n_op - 1, start + width, MR + width, sems.at[2])
    middle.wait()
    for piece, left in enumerate(lefts):
        for inner in range(terms):
            offset = pl.multiple_of((1 + shift[piece, inner]) * MR, MR)
            for v in range(VECS):
                z_ref[piece * terms + inner, v] = jnp.dot(
                    left[inner], window[v, :, pl.ds(offset, width)], preferred_element_type=jnp.float32
                ).astype(jnp.bfloat16)


def left_products(place, shift, lefts, wave, n_op):
    terms = lefts[0].shape[0]
    width = wave.shape[2] // n_op
    z_shape = (n_op * terms, VECS, ML, width)
    return pl.pallas_call(
        functools.partial(left_kernel, n_op),
        out_shape=jax.ShapeDtypeStruct(z_shape, jnp.bfloat16),
        in_specs=[pl.BlockSpec(memory_space=pltpu.SMEM)] * 2
        + [pl.BlockSpec(memory_space=pltpu.VMEM)] * n_op
        + [pl.BlockSpec(memory_space=pl.ANY)],
        out_specs=pl.BlockSpec(memory_space=pltpu.VMEM),
        scratch_shapes=[pltpu.VMEM((VECS, ML, width + 2 * MR), jnp.bfloat16), pltpu.SemaphoreType.DMA((3,))],
        compiler_params=pltpu.CompilerParams(vmem_limit_bytes=VMEM_BYTES),
        cost_estimate=pl.CostEstimate(
            flops=2 * n_op * terms * VECS * ML * ML * width, bytes_accessed=8 * 1024 * 1024, transcendentals=0
        ),
        name="left_products",
    )(place, shift, *lefts, wave)


def right_kernel(cls, per, place, shift, z_any, mine, theirs, zero_ref, up_ref, down_ref, z_cols, total, sem):
    column = pl.multiple_of(((place[1] % per) ^ cls) * MR, MR)
    copy = pltpu.make_async_copy(z_any.at[:, :, :, pl.ds(column, MR)], z_cols, sem)
    copy.start()
    total[...] = jnp.zeros_like(total)
    copy.wait()
    half, terms = mine.shape[0], mine.shape[1]
    for piece in range(2 * half):
        right = mine if piece < half else theirs
        for inner in range(terms):
            total[1 + shift[piece, inner]] += jnp.dot(
                z_cols[piece * terms + inner].reshape(VECS * ML, MR),
                right[piece % half, inner],
                preferred_element_type=jnp.float32,
            ).reshape(VECS, ML, MR)
    zero_ref[...] = total[1]
    up_ref[...] = total[2].astype(jnp.bfloat16)
    down_ref[...] = total[0].astype(jnp.bfloat16)


def right_products(cls, per, place, shift, z, mine, theirs):
    block = (VECS, ML, MR)
    vmem = pl.BlockSpec(memory_space=pltpu.VMEM)
    smem = pl.BlockSpec(memory_space=pltpu.SMEM)
    return pl.pallas_call(
        functools.partial(right_kernel, cls, per),
        out_shape=[
            jax.ShapeDtypeStruct(block, jnp.float32),
            jax.ShapeDtypeStruct(block, jnp.bfloat16),
            jax.ShapeDtypeStruct(block, jnp.bfloat16),
        ],
        in_specs=[smem, smem, pl.BlockSpec(memory_space=pl.ANY), vmem, vmem],
        out_specs=[vmem] * 3,
        scratch_shapes=[
            pltpu.VMEM((z.shape[0],) + block, jnp.bfloat16),
            pltpu.VMEM((3,) + block, jnp.float32),
            pltpu.SemaphoreType.DMA,
        ],
        compiler_params=pltpu.CompilerParams(vmem_limit_bytes=VMEM_BYTES),
        cost_estimate=pl.CostEstimate(
            flops=2 * z.shape[0] * VECS * ML * MR * MR, bytes_accessed=4 * 1024 * 1024, transcendentals=0
        ),
        name="right_products",
    )(place, shift, z, mine, theirs)


def sum_kernel(per, place, *refs):
    *parts, out_ref, total = refs
    sec = place[1]
    total[...] = jnp.zeros_like(total)
    for index, part in enumerate(parts):
        cls, kind = divmod(index, 3)
        source = sec if kind == 0 else (sec + per - 1 if kind == 1 else sec + 1)
        column = pl.multiple_of(((source % per) ^ cls) * MR, MR)
        total[:, :, pl.ds(column, MR)] += part[...].astype(jnp.float32)
    out_ref[...] = total[...].astype(jnp.bfloat16)


def summed(per, place, parts):
    shape = (VECS, ML, per * MR)
    vmem = pl.BlockSpec(memory_space=pltpu.VMEM)
    return pl.pallas_call(
        functools.partial(sum_kernel, per),
        out_shape=jax.ShapeDtypeStruct(shape, jnp.bfloat16),
        in_specs=[pl.BlockSpec(memory_space=pltpu.SMEM)] + [vmem] * len(parts),
        out_specs=vmem,
        scratch_shapes=[pltpu.VMEM(shape, jnp.float32)],
        compiler_params=pltpu.CompilerParams(vmem_limit_bytes=VMEM_BYTES),
        name="summed",
    )(place, *parts)


def on_device(n_op, n_sec, wavefunction, left_ops, right_ops, term_shift):
    per = n_sec // n_op
    place = jnp.stack([lax.axis_index("op"), lax.axis_index("sec")]).astype(jnp.int32)
    wave = wavefunction.transpose(1, 0, 2)
    lefts = doubled(left_ops.transpose(1, 0, 2), n_op)
    rights = right_classes(right_ops, n_op, n_sec)
    shift = shifts_of(term_shift, n_op)
    z = left_products(place, shift, lefts, wave, n_op)
    forward = [(d, d + 1) for d in range(n_sec - 1)]
    backward = [(d + 1, d) for d in range(n_sec - 1)]
    parts = []
    for cls, (mine, theirs) in enumerate(rights):
        zero, up, down = right_products(cls, per, place, shift, z, mine, theirs)
        parts += [zero, lax.ppermute(up, "sec", forward), lax.ppermute(down, "sec", backward)]
    return summed(per, place, parts).transpose(1, 0, 2)


def solution(mesh):
    in_specs = (P("sec", None, None), P("sec", "op", None), P("op", "sec", None, None), P("op"))
    out_specs = P("sec", None, "op")
    return jax.shard_map(
        functools.partial(on_device, mesh.shape["op"], mesh.shape["sec"]),
        mesh=mesh,
        in_specs=in_specs,
        out_specs=out_specs,
        check_vma=False,
    )
```

```python
import functools

import jax
import jax.numpy as jnp
from jax import lax
from jax.experimental import pallas as pl
from jax.experimental.pallas import tpu as pltpu
from jax.sharding import PartitionSpec as P

ML = 256
MR = 128
VECS = 3
TILE = 16
SMEM = pl.BlockSpec(memory_space=pltpu.SMEM)
VMEM = pl.BlockSpec(memory_space=pltpu.VMEM)
HBM = pl.BlockSpec(memory_space=pltpu.HBM)


def in_vmem(shape, dtype=jnp.bfloat16):
    return pltpu.VMEM(shape, dtype)


def grant(mebibytes):
    return pltpu.CompilerParams(vmem_limit_bytes=mebibytes * 1024 * 1024)


def over_op(x, n_op, bit):
    return lax.ppermute(x, "op", [(o, o ^ bit) for o in range(n_op)])


def over_sec(x, n_sec, bit):
    return lax.ppermute(x, "sec", [(d, d ^ bit) for d in range(n_sec)])


def right_first(held, n_op, n_sec, bit):
    per = n_sec // n_op
    first, second = [], []
    for o in range(n_op):
        for d in range(n_sec):
            source = o * n_sec + d
            if (o & bit) == ((d // per) & bit):
                first.append((source, o * n_sec + (d ^ (bit * per))))
            else:
                first.append((source, (o ^ bit) * n_sec + d))
                second.append((source, (o ^ bit) * n_sec + (d ^ (bit * per))))
    return lax.ppermute(held, ("op", "sec"), first), lax.ppermute(held, ("op", "sec"), second)


def pack_kernel(n_op, place, shift, left, wave, packed, window, sems):
    terms = left.shape[0]
    width = window.shape[2] - 2 * MR
    op = place[0]
    start = pl.multiple_of(op * width, MR)
    copies = [
        pltpu.make_async_copy(wave.at[:, :, pl.ds(start, width)], window.at[:, :, pl.ds(MR, width)], sems.at[0]),
        pltpu.make_async_copy(left, packed.at[:, pl.ds(0, ML)], sems.at[1]),
    ]
    for copy in copies:
        copy.start()

    def edge(valid, source, target, sem):
        @pl.when(valid)
        def _():
            copy = pltpu.make_async_copy(
                wave.at[:, :, pl.ds(pl.multiple_of(source, MR), MR)], window.at[:, :, pl.ds(target, MR)], sem
            )
            copy.start()
            copy.wait()

        @pl.when(jnp.logical_not(valid))
        def _():
            window[:, :, pl.ds(target, MR)] = jnp.zeros((VECS, ML, MR), jnp.bfloat16)

    for inner in range(terms):
        packed[inner, ML:] = jnp.full((TILE, ML), shift[inner].astype(jnp.float32)).astype(jnp.bfloat16)
    edge(op > 0, start - MR, 0, sems.at[2])
    edge(op < n_op - 1, start + width, MR + width, sems.at[3])
    for copy in copies:
        copy.wait()


def pack(place, shift, left, wave, n_op):
    width = wave.shape[2] // n_op
    return pl.pallas_call(
        functools.partial(pack_kernel, n_op),
        out_shape=[in_vmem((left.shape[0], ML + TILE, ML)), in_vmem((VECS, ML, width + 2 * MR))],
        in_specs=[SMEM, SMEM, HBM, HBM],
        out_specs=[VMEM] * 2,
        scratch_shapes=[pltpu.SemaphoreType.DMA((4,))],
        compiler_params=grant(8),
        cost_estimate=pl.CostEstimate(flops=0, bytes_accessed=32 * 1024 * 1024, transcendentals=0),
        name="pack",
    )(place, shift, pltpu.with_memory_space_constraint(left, pltpu.HBM), pltpu.with_memory_space_constraint(wave, pltpu.HBM))


def left_kernel(*refs):
    *lefts, window, z_ref, shift_ref = refs
    per = z_ref.shape[0]
    width = per * MR
    terms = lefts[0].shape[0]
    for piece, left in enumerate(lefts):
        for inner in range(terms):
            term = piece * terms + inner
            shift = jnp.max(left[inner, ML:, :MR].astype(jnp.float32)).astype(jnp.int32)
            shift_ref[term] = shift
            offset = pl.multiple_of((1 + shift) * MR, MR)
            for v in range(VECS):
                z = jnp.dot(
                    left[inner, :ML], window[v, :, pl.ds(offset, width)], preferred_element_type=jnp.float32
                ).astype(jnp.bfloat16)
                for column in range(per):
                    z_ref[column, v, :, term * MR : (term + 1) * MR] = z[:, column * MR : (column + 1) * MR]


def left_products(lefts, window):
    terms = len(lefts) * lefts[0].shape[0]
    width = window.shape[2] - 2 * MR
    return pl.pallas_call(
        left_kernel,
        out_shape=[in_vmem((width // MR, VECS, ML, terms * MR)), jax.ShapeDtypeStruct((terms,), jnp.int32)],
        in_specs=[VMEM] * (len(lefts) + 1),
        out_specs=[VMEM, SMEM],
        compiler_params=grant(8 + 4 * width // MR),
        cost_estimate=pl.CostEstimate(
            flops=2 * terms * VECS * ML * ML * width, bytes_accessed=1024 * 1024, transcendentals=0
        ),
        name="left_products",
    )(*lefts, window)


def right_kernel(cls, per, place, shift, z_ref, own, other, received, zero_ref, up_ref, down_ref, right):
    column = (place[1] % per) ^ cls
    same = place[2] == 1
    half, terms = own.shape[0], own.shape[1]
    for piece in range(2 * half):
        for inner in range(terms):
            term = piece * terms + inner
            if piece < half:
                block = jnp.where(same, own[piece, inner], other[piece, inner])
            else:
                block = received[piece - half, inner]
            for kind in range(3):
                right[term * MR : (term + 1) * MR, kind * MR : (kind + 1) * MR] = jnp.where(
                    shift[term] == kind - 1, block, jnp.zeros_like(block)
                )
    for v in range(VECS):
        y = jnp.dot(z_ref[column, v], right[...], preferred_element_type=jnp.float32)
        down_ref[v] = y[:, :MR].astype(jnp.bfloat16)
        zero_ref[v] = y[:, MR : 2 * MR]
        up_ref[v] = y[:, 2 * MR :].astype(jnp.bfloat16)


def right_products(cls, per, place, shift, z, own, other, received):
    block = (VECS, ML, MR)
    depth = z.shape[3]
    return pl.pallas_call(
        functools.partial(right_kernel, cls, per),
        out_shape=[jax.ShapeDtypeStruct(block, dtype) for dtype in (jnp.float32, jnp.bfloat16, jnp.bfloat16)],
        in_specs=[SMEM, SMEM] + [VMEM] * 4,
        out_specs=[VMEM] * 3,
        scratch_shapes=[in_vmem((depth, 3 * MR))],
        compiler_params=grant(16),
        cost_estimate=pl.CostEstimate(flops=0, bytes_accessed=0, transcendentals=0),
        name="right_products",
    )(place, shift, z, own, other, received)


def sum_kernel(per, place, *refs):
    *parts, out_ref = refs
    zeros, ups, downs = parts[::3], parts[1::3], parts[2::3]
    sec = place[1]
    below, above = (sec ^ (sec + per - 1)) % per, (sec ^ (sec + 1)) % per

    def add(low, high):
        @pl.when((below == low) & (above == high))
        def _():
            for cls in range(per):
                column = pl.multiple_of(((sec % per) ^ cls) * MR, MR)
                for v in range(VECS):
                    total = zeros[cls][v] + ups[cls ^ low][v].astype(jnp.float32)
                    total = total + downs[cls ^ high][v].astype(jnp.float32)
                    out_ref[v, :, pl.ds(column, MR)] = total.astype(jnp.bfloat16)

    carry = 1
    while carry < per:
        add(1, carry)
        if carry > 1:
            add(carry, 1)
        carry = 2 * carry + 1


def summed(per, place, parts):
    return pl.pallas_call(
        functools.partial(sum_kernel, per),
        out_shape=jax.ShapeDtypeStruct((VECS, ML, per * MR), jnp.bfloat16),
        in_specs=[SMEM] + [VMEM] * len(parts),
        out_specs=VMEM,
        compiler_params=grant(16),
        name="summed",
    )(place, *parts)


def on_device(n_op, n_sec, wavefunction, left_ops, right_ops, term_shift):
    per = n_sec // n_op
    tie = lax.optimization_barrier
    op, sec = lax.axis_index("op"), lax.axis_index("sec")
    matching = op ^ (sec // per)
    place = jnp.stack([op, sec, (matching & 1) ^ 1]).astype(jnp.int32)
    held = right_ops.reshape((1,) + right_ops.shape[:1] + right_ops.shape[2:])
    packed, window = pack(place, term_shift, left_ops.transpose(1, 0, 2), wavefunction.transpose(1, 0, 2), n_op)
    lefts = [packed]
    bit = n_op // 2
    while bit > 1:
        one, two = tie(right_first(held, n_op, n_sec, bit))
        same = (matching & bit) == 0
        held = jnp.concatenate([jnp.where(same, held, one), jnp.where(same, one, two)])
        lefts = lefts + [over_op(x, n_op, bit) for x in lefts]
        bit //= 2
    lefts = lefts + [over_op(x, n_op, 1) for x in lefts]
    owns = [held]
    bit = 1
    while bit < per:
        owns = owns + [over_sec(c, n_sec, bit) for c in owns]
        bit *= 2
    other, owns = tie((over_sec(owns[0], n_sec, per), owns))
    z, shift = left_products(lefts, window)
    forward = [(d, d + 1) for d in range(n_sec - 1)]
    backward = [(d + 1, d) for d in range(n_sec - 1)]
    same = (matching & 1) == 0
    parts = []
    for cls, own in enumerate(owns):
        received = over_op(jnp.where(same, other, own), n_op, 1)
        later = over_sec(owns[cls + 1], n_sec, per) if cls + 1 < per else None
        zero, up, down = right_products(cls, per, place, shift, z, own, other, received)
        parts += [zero, lax.ppermute(up, "sec", forward), lax.ppermute(down, "sec", backward)]
        if later is not None:
            other, _ = tie((later, up))
    return summed(per, place, parts).transpose(1, 0, 2)


def solution(mesh):
    in_specs = (P("sec", None, None), P("sec", "op", None), P("op", "sec", None, None), P("op"))
    out_specs = P("sec", None, "op")
    return jax.shard_map(
        functools.partial(on_device, mesh.shape["op"], mesh.shape["sec"]),
        mesh=mesh,
        in_specs=in_specs,
        out_specs=out_specs,
        check_vma=False,
    )
```

```python
import functools

import jax
import jax.numpy as jnp
from jax import lax
from jax.experimental import pallas as pl
from jax.experimental.pallas import tpu as pltpu
from jax.sharding import PartitionSpec as P

ML = 256
MR = 128
VECS = 3
TILE = 16
VMEM = pl.BlockSpec(memory_space=pltpu.VMEM)
HBM = pl.BlockSpec(memory_space=pltpu.HBM)


def in_vmem(shape, dtype=jnp.bfloat16):
    return pltpu.VMEM(shape, dtype)


def in_hbm(x):
    return pltpu.with_memory_space_constraint(x, pltpu.HBM)


def grant(mebibytes):
    return pltpu.CompilerParams(vmem_limit_bytes=mebibytes * 1024 * 1024)


def cost(flops, bytes_accessed):
    return pl.CostEstimate(flops=flops, bytes_accessed=bytes_accessed, transcendentals=0)


def over_op(x, n_op, bit):
    return lax.ppermute(x, "op", [(o, o ^ bit) for o in range(n_op)])


def over_sec(x, n_sec, bit):
    return lax.ppermute(x, "sec", [(d, d ^ bit) for d in range(n_sec)])


def on_own_side(per, bit):
    return ((lax.axis_index("op") ^ (lax.axis_index("sec") // per)) & bit) == 0


def towards_owner(held, n_op, n_sec, bit):
    per = n_sec // n_op
    first, second = [], []
    for o in range(n_op):
        for d in range(n_sec):
            source = o * n_sec + d
            far = d ^ (bit * per)
            if (o & bit) == ((d // per) & bit):
                first.append((source, o * n_sec + far))
            else:
                first.append((source, (o ^ bit) * n_sec + d))
                second.append((source, (o ^ bit) * n_sec + far))
    return lax.ppermute(held, ("op", "sec"), first), lax.ppermute(held, ("op", "sec"), second)


def route_kernel(per, bit, held, one, two, out_ref):
    half = held.shape[0]
    own = on_own_side(per, bit)
    out_ref[:half] = jnp.where(own, held[...], one[...])
    out_ref[half:] = jnp.where(own, one[...], two[...])


def route(held, one, two, per, bit):
    return pl.pallas_call(
        functools.partial(route_kernel, per, bit),
        out_shape=in_vmem((2 * held.shape[0],) + held.shape[1:]),
        in_specs=[VMEM] * 3,
        out_specs=VMEM,
        compiler_params=grant(4),
        cost_estimate=cost(0, 0),
        name="route",
    )(held, one, two)


def pick_kernel(per, own, other, out_ref):
    out_ref[...] = jnp.where(on_own_side(per, 1), other[...], own[...])


def pick(own, other, per):
    return pl.pallas_call(
        functools.partial(pick_kernel, per),
        out_shape=in_vmem(own.shape),
        in_specs=[VMEM] * 2,
        out_specs=VMEM,
        compiler_params=grant(4),
        cost_estimate=cost(0, 0),
        name="pick",
    )(own, other)


def shift_of(left, inner):
    return jnp.max(left[inner, ML:, :MR].astype(jnp.float32)).astype(jnp.int32)


def pack_kernel(n_op, shift, left, wave, packed, window, shift_ref, sems):
    width = window.shape[2] - 2 * MR
    op = lax.axis_index("op")
    start = pl.multiple_of(op * width, MR)
    copies = [
        pltpu.make_async_copy(shift, shift_ref, sems.at[0]),
        pltpu.make_async_copy(left, packed.at[:, pl.ds(0, ML)], sems.at[1]),
        pltpu.make_async_copy(wave.at[:, :, pl.ds(start, width)], window.at[:, :, pl.ds(MR, width)], sems.at[2]),
    ]
    for copy in copies:
        copy.start()

    def edge(valid, source, target, sem):
        @pl.when(valid)
        def _():
            copy = pltpu.make_async_copy(
                wave.at[:, :, pl.ds(pl.multiple_of(source, MR), MR)], window.at[:, :, pl.ds(target, MR)], sem
            )
            copy.start()
            copy.wait()

        @pl.when(jnp.logical_not(valid))
        def _():
            window[:, :, pl.ds(target, MR)] = jnp.zeros((VECS, ML, MR), jnp.bfloat16)

    edge(op > 0, start - MR, 0, sems.at[3])
    edge(op < n_op - 1, start + width, MR + width, sems.at[4])
    copies[0].wait()
    for inner in range(left.shape[0]):
        tag = jnp.full((TILE, ML), shift_ref[inner].astype(jnp.float32)).astype(jnp.bfloat16)
        packed[inner, ML:] = tag
    copies[1].wait()
    copies[2].wait()


def pack(shift, left, wave, n_op):
    width = wave.shape[2] // n_op
    return pl.pallas_call(
        functools.partial(pack_kernel, n_op),
        out_shape=[in_vmem((left.shape[0], ML + TILE, ML)), in_vmem((VECS, ML, width + 2 * MR))],
        in_specs=[HBM] * 3,
        out_specs=[VMEM] * 2,
        scratch_shapes=[pltpu.SMEM(shift.shape, jnp.int32), pltpu.SemaphoreType.DMA((5,))],
        compiler_params=grant(8),
        cost_estimate=cost(0, 32 * 1024 * 1024),
        name="pack",
    )(in_hbm(shift), in_hbm(left), in_hbm(wave))


def left_kernel(*refs):
    *lefts, window, z_ref = refs
    per = z_ref.shape[0]
    width = per * MR
    terms = lefts[0].shape[0]
    for piece, left in enumerate(lefts):
        for inner in range(terms):
            term = piece * terms + inner
            offset = pl.multiple_of((1 + shift_of(left, inner)) * MR, MR)
            for v in range(VECS):
                z = jnp.dot(
                    left[inner, :ML], window[v, :, pl.ds(offset, width)], preferred_element_type=jnp.float32
                ).astype(jnp.bfloat16)
                for column in range(per):
                    z_ref[column, v, :, term * MR : (term + 1) * MR] = z[:, column * MR : (column + 1) * MR]


def left_products(lefts, window):
    terms = len(lefts) * lefts[0].shape[0]
    width = window.shape[2] - 2 * MR
    return pl.pallas_call(
        left_kernel,
        out_shape=in_vmem((width // MR, VECS, ML, terms * MR)),
        in_specs=[VMEM] * (len(lefts) + 1),
        out_specs=VMEM,
        compiler_params=grant(8 + 4 * width // MR),
        cost_estimate=cost(2 * terms * VECS * ML * ML * width, 1024 * 1024),
        name="left_products",
    )(*lefts, window)


def right_kernel(cls, per, z_ref, own, other, received, *refs):
    *lefts, zero_ref, low_ref, high_ref, total = refs
    sec = lax.axis_index("sec")
    column = (sec % per) ^ cls
    even = sec % 2 == 0
    settled = on_own_side(per, 1)
    half, terms = own.shape[0], own.shape[1]
    total[...] = jnp.zeros_like(total)
    for piece, left in enumerate(lefts):
        for inner in range(terms):
            term = piece * terms + inner
            kind = 1 + shift_of(left, inner)
            if piece < half:
                block = jnp.where(settled, own[piece, inner], other[piece, inner])
            else:
                block = received[piece - half, inner]
            for v in range(VECS):
                total[kind, v] += jnp.dot(
                    z_ref[column, v, :, term * MR : (term + 1) * MR], block, preferred_element_type=jnp.float32
                )
    for v in range(VECS):
        down, up = total[0, v].astype(jnp.bfloat16), total[2, v].astype(jnp.bfloat16)
        zero_ref[v] = total[1, v]
        low_ref[v] = jnp.where(even, up, down)
        high_ref[v] = jnp.where(even, down, up)


def right_products(cls, per, z, own, other, received, lefts):
    block = (VECS, ML, MR)
    return pl.pallas_call(
        functools.partial(right_kernel, cls, per),
        out_shape=[jax.ShapeDtypeStruct(block, dtype) for dtype in (jnp.float32, jnp.bfloat16, jnp.bfloat16)],
        in_specs=[VMEM] * (4 + len(lefts)),
        out_specs=[VMEM] * 3,
        scratch_shapes=[in_vmem((3,) + block, jnp.float32)],
        compiler_params=grant(8),
        cost_estimate=cost(0, 0),
        name="right_products",
    )(z, own, other, received, *lefts)


def sum_kernel(per, *refs):
    *parts, out_ref = refs
    zeros, lows, highs = parts[::3], parts[1::3], parts[2::3]
    sec = lax.axis_index("sec")
    beyond = (sec ^ ((((sec + 1) ^ 1) + per - 1) % per)) % per

    def add(high):
        @pl.when(beyond == high)
        def _():
            for cls in range(per):
                column = pl.multiple_of(((sec % per) ^ cls) * MR, MR)
                for v in range(VECS):
                    total = zeros[cls][v] + lows[cls ^ 1][v].astype(jnp.float32)
                    total = total + highs[cls ^ high][v].astype(jnp.float32)
                    out_ref[v, :, pl.ds(column, MR)] = total.astype(jnp.bfloat16)

    carry = 1
    while carry < per:
        add(carry)
        carry = 2 * carry + 1


def summed(per, parts):
    return pl.pallas_call(
        functools.partial(sum_kernel, per),
        out_shape=jax.ShapeDtypeStruct((VECS, ML, per * MR), jnp.bfloat16),
        in_specs=[VMEM] * len(parts),
        out_specs=VMEM,
        compiler_params=grant(8),
        name="summed",
    )(*parts)


def on_device(n_op, n_sec, wavefunction, left_ops, right_ops, term_shift):
    per = n_sec // n_op
    tie = lax.optimization_barrier
    matching = lax.axis_index("op") ^ (lax.axis_index("sec") // per)
    held = right_ops.reshape((1,) + right_ops.shape[:1] + right_ops.shape[2:])
    packed, window = pack(term_shift, left_ops.transpose(1, 0, 2), wavefunction.transpose(1, 0, 2), n_op)
    lefts = [packed]
    bit = n_op // 2
    while bit > 1:
        one, two = tie(towards_owner(held, n_op, n_sec, bit))
        same = (matching & bit) == 0
        held = jnp.concatenate([jnp.where(same, held, one), jnp.where(same, one, two)])
        lefts = lefts + [over_op(x, n_op, bit) for x in lefts]
        bit //= 2
    lefts = lefts + [over_op(x, n_op, 1) for x in lefts]
    owns = [held]
    bit = 1
    while bit < per:
        owns = owns + [over_sec(c, n_sec, bit) for c in owns]
        bit *= 2
    other, owns = tie((over_sec(owns[0], n_sec, per), owns))
    z = left_products(lefts, window)
    low = [(d, d ^ 1) for d in range(n_sec)]
    high = [(d, ((d + 1) ^ 1) - 1) for d in range(1, n_sec - 1)]
    settled = (matching & 1) == 0
    parts = []
    for cls, own in enumerate(owns):
        received = over_op(jnp.where(settled, other, own), n_op, 1)
        later = over_sec(owns[cls + 1], n_sec, per) if cls + 1 < per else None
        zero, to_low, to_high = right_products(cls, per, z, own, other, received, lefts)
        parts += [zero, lax.ppermute(to_low, "sec", low), lax.ppermute(to_high, "sec", high)]
        if later is not None:
            other, _ = tie((later, zero))
    return summed(per, parts).transpose(1, 0, 2)


def solution(mesh):
    in_specs = (P("sec", None, None), P("sec", "op", None), P("op", "sec", None, None), P("op"))
    out_specs = P("sec", None, "op")
    return jax.shard_map(
        functools.partial(on_device, mesh.shape["op"], mesh.shape["sec"]),
        mesh=mesh,
        in_specs=in_specs,
        out_specs=out_specs,
        check_vma=False,
    )
```

```python
import functools

import jax
import jax.numpy as jnp
from jax import lax
from jax.experimental import pallas as pl
from jax.experimental.pallas import tpu as pltpu
from jax.sharding import PartitionSpec as P

ML = 256
MR = 128
VECS = 3
TILE = 16
VMEM = pl.BlockSpec(memory_space=pltpu.VMEM)
HBM = pl.BlockSpec(memory_space=pltpu.HBM)


def in_vmem(shape, dtype=jnp.bfloat16):
    return pltpu.VMEM(shape, dtype)


def in_hbm(x):
    return pltpu.with_memory_space_constraint(x, pltpu.HBM)


def grant(mebibytes):
    return pltpu.CompilerParams(vmem_limit_bytes=mebibytes * 1024 * 1024)


def cost(flops, bytes_accessed):
    return pl.CostEstimate(flops=flops, bytes_accessed=bytes_accessed, transcendentals=0)


def over_op(x, n_op, bit):
    return lax.ppermute(x, "op", [(o, o ^ bit) for o in range(n_op)])


def over_sec(x, n_sec, bit):
    return lax.ppermute(x, "sec", [(d, d ^ bit) for d in range(n_sec)])


def on_own_side(per, bit):
    return ((lax.axis_index("op") ^ (lax.axis_index("sec") // per)) & bit) == 0


def towards_owner(held, n_op, n_sec, bit):
    per = n_sec // n_op
    first, second = [], []
    for o in range(n_op):
        for d in range(n_sec):
            source = o * n_sec + d
            far = d ^ (bit * per)
            if (o & bit) == ((d // per) & bit):
                first.append((source, o * n_sec + far))
            else:
                first.append((source, (o ^ bit) * n_sec + d))
                second.append((source, (o ^ bit) * n_sec + far))
    return lax.ppermute(held, ("op", "sec"), first), lax.ppermute(held, ("op", "sec"), second)


def route_kernel(per, bit, held, one, two, out_ref):
    half = held.shape[0]
    own = on_own_side(per, bit)
    out_ref[:half] = jnp.where(own, held[...], one[...])
    out_ref[half:] = jnp.where(own, one[...], two[...])


def route(held, one, two, per, bit):
    return pl.pallas_call(
        functools.partial(route_kernel, per, bit),
        out_shape=in_vmem((2 * held.shape[0],) + held.shape[1:]),
        in_specs=[VMEM] * 3,
        out_specs=VMEM,
        compiler_params=grant(4),
        cost_estimate=cost(0, 0),
        name="route",
    )(held, one, two)


def pick_kernel(per, own, other, out_ref):
    out_ref[...] = jnp.where(on_own_side(per, 1), other[...], own[...])


def pick(own, other, per):
    return pl.pallas_call(
        functools.partial(pick_kernel, per),
        out_shape=in_vmem(own.shape),
        in_specs=[VMEM] * 2,
        out_specs=VMEM,
        compiler_params=grant(4),
        cost_estimate=cost(0, 0),
        name="pick",
    )(own, other)


def shift_of(left, inner):
    return jnp.max(left[inner, ML:, :MR].astype(jnp.float32)).astype(jnp.int32)


def pack_kernel(shift, left, right, packed, kept, shift_ref, sems):
    copies = [
        pltpu.make_async_copy(shift, shift_ref, sems.at[0]),
        pltpu.make_async_copy(left, packed.at[:, pl.ds(0, ML)], sems.at[1]),
        pltpu.make_async_copy(right, kept, sems.at[2]),
    ]
    for copy in copies:
        copy.start()
    copies[0].wait()
    for inner in range(left.shape[0]):
        tag = jnp.full((TILE, ML), shift_ref[inner].astype(jnp.float32)).astype(jnp.bfloat16)
        packed[inner, ML:] = tag
    for copy in copies[1:]:
        copy.wait()


def pack(shift, left, right):
    return pl.pallas_call(
        pack_kernel,
        out_shape=[in_vmem((left.shape[0], ML + TILE, ML)), in_vmem(right.shape)],
        in_specs=[HBM] * 3,
        out_specs=[VMEM] * 2,
        scratch_shapes=[pltpu.SMEM(shift.shape, jnp.int32), pltpu.SemaphoreType.DMA((3,))],
        compiler_params=grant(8),
        cost_estimate=cost(0, 32 * 1024 * 1024),
        name="pack",
    )(in_hbm(shift), in_hbm(left), in_hbm(right))


def window_kernel(n_op, wave, window, sems):
    width = window.shape[2] - 2 * MR
    op = lax.axis_index("op")
    start = pl.multiple_of(op * width, MR)
    middle = pltpu.make_async_copy(
        wave.at[:, :, pl.ds(start, width)], window.at[:, :, pl.ds(MR, width)], sems.at[0]
    )
    middle.start()

    def edge(valid, source, target, sem):
        @pl.when(valid)
        def _():
            copy = pltpu.make_async_copy(
                wave.at[:, :, pl.ds(pl.multiple_of(source, MR), MR)], window.at[:, :, pl.ds(target, MR)], sem
            )
            copy.start()
            copy.wait()

        @pl.when(jnp.logical_not(valid))
        def _():
            window[:, :, pl.ds(target, MR)] = jnp.zeros((VECS, ML, MR), jnp.bfloat16)

    edge(op > 0, start - MR, 0, sems.at[1])
    edge(op < n_op - 1, start + width, MR + width, sems.at[2])
    middle.wait()


def window_of(wave, n_op):
    width = wave.shape[2] // n_op
    return pl.pallas_call(
        functools.partial(window_kernel, n_op),
        out_shape=in_vmem((VECS, ML, width + 2 * MR)),
        in_specs=[HBM],
        out_specs=VMEM,
        scratch_shapes=[pltpu.SemaphoreType.DMA((3,))],
        compiler_params=grant(4),
        cost_estimate=cost(0, 2 * 1024 * 1024),
        name="window",
    )(in_hbm(wave))


def left_kernel(*refs):
    *lefts, window, z_ref = refs
    per = z_ref.shape[0]
    width = per * MR
    terms = lefts[0].shape[0]
    for piece, left in enumerate(lefts):
        for inner in range(terms):
            term = piece * terms + inner
            offset = pl.multiple_of((1 + shift_of(left, inner)) * MR, MR)
            for v in range(VECS):
                z = jnp.dot(
                    left[inner, :ML], window[v, :, pl.ds(offset, width)], preferred_element_type=jnp.float32
                ).astype(jnp.bfloat16)
                for column in range(per):
                    z_ref[column, v, :, term * MR : (term + 1) * MR] = z[:, column * MR : (column + 1) * MR]


def left_products(lefts, window):
    terms = len(lefts) * lefts[0].shape[0]
    width = window.shape[2] - 2 * MR
    return pl.pallas_call(
        left_kernel,
        out_shape=in_vmem((width // MR, VECS, ML, terms * MR)),
        in_specs=[VMEM] * (len(lefts) + 1),
        out_specs=VMEM,
        compiler_params=grant(8 + 4 * width // MR),
        cost_estimate=cost(2 * terms * VECS * ML * ML * width, 1024 * 1024),
        name="left_products",
    )(*lefts, window)


def right_kernel(cls, per, z_ref, own, other, received, *refs):
    *lefts, zero_ref, low_ref, high_ref, total = refs
    sec = lax.axis_index("sec")
    column = (sec % per) ^ cls
    even = sec % 2 == 0
    settled = on_own_side(per, 1)
    half, terms = own.shape[0], own.shape[1]
    total[...] = jnp.zeros_like(total)
    for piece, left in enumerate(lefts):
        for inner in range(terms):
            term = piece * terms + inner
            kind = 1 + shift_of(left, inner)
            if piece < half:
                block = jnp.where(settled, own[piece, inner], other[piece, inner])
            else:
                block = received[piece - half, inner]
            for v in range(VECS):
                total[kind, v] += jnp.dot(
                    z_ref[column, v, :, term * MR : (term + 1) * MR], block, preferred_element_type=jnp.float32
                )
    for v in range(VECS):
        down, up = total[0, v].astype(jnp.bfloat16), total[2, v].astype(jnp.bfloat16)
        zero_ref[v] = total[1, v]
        low_ref[v] = jnp.where(even, up, down)
        high_ref[v] = jnp.where(even, down, up)


def right_products(cls, per, z, own, other, received, lefts):
    block = (VECS, ML, MR)
    return pl.pallas_call(
        functools.partial(right_kernel, cls, per),
        out_shape=[jax.ShapeDtypeStruct(block, dtype) for dtype in (jnp.float32, jnp.bfloat16, jnp.bfloat16)],
        in_specs=[VMEM] * (4 + len(lefts)),
        out_specs=[VMEM] * 3,
        scratch_shapes=[in_vmem((3,) + block, jnp.float32)],
        compiler_params=grant(8),
        cost_estimate=cost(0, 0),
        name="right_products",
    )(z, own, other, received, *lefts)


def sum_kernel(per, *refs):
    *parts, out_ref = refs
    zeros, lows, highs = parts[::3], parts[1::3], parts[2::3]
    sec = lax.axis_index("sec")
    beyond = (sec ^ ((((sec + 1) ^ 1) + per - 1) % per)) % per

    def add(high):
        @pl.when(beyond == high)
        def _():
            for cls in range(per):
                column = pl.multiple_of(((sec % per) ^ cls) * MR, MR)
                for v in range(VECS):
                    total = zeros[cls][v] + lows[cls ^ 1][v].astype(jnp.float32)
                    total = total + highs[cls ^ high][v].astype(jnp.float32)
                    out_ref[v, :, pl.ds(column, MR)] = total.astype(jnp.bfloat16)

    carry = 1
    while carry < per:
        add(carry)
        carry = 2 * carry + 1


def summed(per, parts):
    return pl.pallas_call(
        functools.partial(sum_kernel, per),
        out_shape=jax.ShapeDtypeStruct((VECS, ML, per * MR), jnp.bfloat16),
        in_specs=[VMEM] * len(parts),
        out_specs=VMEM,
        compiler_params=grant(8),
        name="summed",
    )(*parts)


def on_device(n_op, n_sec, wavefunction, left_ops, right_ops, term_shift):
    per = n_sec // n_op
    tie = lax.optimization_barrier
    matching = lax.axis_index("op") ^ (lax.axis_index("sec") // per)
    held = right_ops.reshape((1,) + right_ops.shape[:1] + right_ops.shape[2:])
    packed, kept = pack(term_shift, left_ops.transpose(1, 0, 2), held)
    window = window_of(wavefunction.transpose(1, 0, 2), n_op)
    lefts = [packed]
    bit = n_op // 2
    while bit > 1:
        one, two, window = tie((*towards_owner(held, n_op, n_sec, bit), window))
        same = (matching & bit) == 0
        held = kept = jnp.concatenate([jnp.where(same, kept, one), jnp.where(same, one, two)])
        lefts = lefts + [over_op(x, n_op, bit) for x in lefts]
        bit //= 2
    lefts = lefts + [over_op(x, n_op, 1) for x in lefts]
    owns = [held]
    bit = 1
    while bit < per:
        owns = owns + [over_sec(c, n_sec, bit) for c in owns]
        bit *= 2
    other, owns = tie((over_sec(owns[0], n_sec, per), owns))
    z = left_products(lefts, window)
    low = [(d, d ^ 1) for d in range(n_sec)]
    high = [(d, ((d + 1) ^ 1) - 1) for d in range(1, n_sec - 1)]
    settled = (matching & 1) == 0
    parts, others = [], [other]
    for cls, own in enumerate(owns):
        received = over_op(jnp.where(settled, other, own), n_op, 1)
        later = None
        if cls + 1 < per:
            half = own.shape[0] // 2
            step = (cls + 1) & -(cls + 1)
            later = [
                over_sec(owns[cls + 1][:half], n_sec, per),
                over_sec(others[(cls + 1) ^ step][half:], n_sec, step),
            ]
        zero, to_low, to_high = right_products(cls, per, z, own, other, received, lefts)
        parts += [zero, lax.ppermute(to_low, "sec", low), lax.ppermute(to_high, "sec", high)]
        if later is not None:
            later, _ = tie((later, zero))
            other = jnp.concatenate(later)
            others.append(other)
    return summed(per, parts).transpose(1, 0, 2)


def solution(mesh):
    in_specs = (P("sec", None, None), P("sec", "op", None), P("op", "sec", None, None), P("op"))
    out_specs = P("sec", None, "op")
    return jax.shard_map(
        functools.partial(on_device, mesh.shape["op"], mesh.shape["sec"]),
        mesh=mesh,
        in_specs=in_specs,
        out_specs=out_specs,
        check_vma=False,
    )
```

```python
import functools

import jax
import jax.numpy as jnp
from jax import lax
from jax.experimental import pallas as pl
from jax.experimental.pallas import tpu as pltpu
from jax.sharding import PartitionSpec as P

ML = 256
MR = 128
VECS = 3
TILE = 16
VMEM = pl.BlockSpec(memory_space=pltpu.VMEM)
HBM = pl.BlockSpec(memory_space=pltpu.HBM)


def in_vmem(shape, dtype=jnp.bfloat16):
    return pltpu.VMEM(shape, dtype)


def in_hbm(x):
    return pltpu.with_memory_space_constraint(x, pltpu.HBM)


def grant(mebibytes):
    return pltpu.CompilerParams(vmem_limit_bytes=mebibytes * 1024 * 1024)


def cost(flops, bytes_accessed):
    return pl.CostEstimate(flops=flops, bytes_accessed=bytes_accessed, transcendentals=0)


def over_op(x, n_op, bit):
    return lax.ppermute(x, "op", [(o, o ^ bit) for o in range(n_op)])


def over_sec(x, n_sec, bit):
    return lax.ppermute(x, "sec", [(d, d ^ bit) for d in range(n_sec)])


def on_own_side(per, bit):
    return ((lax.axis_index("op") ^ (lax.axis_index("sec") // per)) & bit) == 0


def towards_owner(held, n_op, n_sec, bit):
    per = n_sec // n_op
    first, second = [], []
    for o in range(n_op):
        for d in range(n_sec):
            source = o * n_sec + d
            far = d ^ (bit * per)
            if (o & bit) == ((d // per) & bit):
                first.append((source, o * n_sec + far))
            else:
                first.append((source, (o ^ bit) * n_sec + d))
                second.append((source, (o ^ bit) * n_sec + far))
    return lax.ppermute(held, ("op", "sec"), first), lax.ppermute(held, ("op", "sec"), second)


def route_kernel(per, bit, held, one, two, out_ref):
    half = held.shape[0]
    own = on_own_side(per, bit)
    out_ref[:half] = jnp.where(own, held[...], one[...])
    out_ref[half:] = jnp.where(own, one[...], two[...])


def route(held, one, two, per, bit):
    return pl.pallas_call(
        functools.partial(route_kernel, per, bit),
        out_shape=in_vmem((2 * held.shape[0],) + held.shape[1:]),
        in_specs=[VMEM] * 3,
        out_specs=VMEM,
        compiler_params=grant(4),
        cost_estimate=cost(0, 0),
        name="route",
    )(held, one, two)


def pick_kernel(per, own, other, out_ref):
    out_ref[...] = jnp.where(on_own_side(per, 1), other[...], own[...])


def pick(own, other, per):
    return pl.pallas_call(
        functools.partial(pick_kernel, per),
        out_shape=in_vmem(own.shape),
        in_specs=[VMEM] * 2,
        out_specs=VMEM,
        compiler_params=grant(4),
        cost_estimate=cost(0, 0),
        name="pick",
    )(own, other)


def shift_of(left, inner):
    row = left.shape[0] - TILE + inner
    return jnp.max(left[row : row + 1, :MR].astype(jnp.float32)).astype(jnp.int32)


def pack_kernel(shift, left, right, packed, kept, shift_ref, sems):
    rows = left.shape[0]
    copies = [
        pltpu.make_async_copy(shift, shift_ref, sems.at[0]),
        pltpu.make_async_copy(left, packed.at[pl.ds(0, rows)], sems.at[1]),
        pltpu.make_async_copy(right, kept, sems.at[2]),
    ]
    for copy in copies:
        copy.start()
    copies[0].wait()
    row = lax.broadcasted_iota(jnp.int32, (TILE, ML), 0)
    tags = jnp.zeros((TILE, ML), jnp.float32)
    for inner in range(rows // ML):
        tags = jnp.where(row == inner, shift_ref[inner].astype(jnp.float32), tags)
    packed[rows:] = tags.astype(jnp.bfloat16)
    for copy in copies[1:]:
        copy.wait()


def pack(shift, left, right):
    return pl.pallas_call(
        pack_kernel,
        out_shape=[in_vmem((left.shape[0] + TILE, ML)), in_vmem(right.shape)],
        in_specs=[HBM] * 3,
        out_specs=[VMEM] * 2,
        scratch_shapes=[pltpu.SMEM(shift.shape, jnp.int32), pltpu.SemaphoreType.DMA((3,))],
        compiler_params=grant(8),
        cost_estimate=cost(0, 32 * 1024 * 1024),
        name="pack",
    )(in_hbm(shift), in_hbm(left), in_hbm(right))


def window_kernel(n_op, wave, window, sems):
    width = window.shape[2] - 2 * MR
    op = lax.axis_index("op")
    start = pl.multiple_of(op * width, MR)
    middle = pltpu.make_async_copy(
        wave.at[:, :, pl.ds(start, width)], window.at[:, :, pl.ds(MR, width)], sems.at[0]
    )
    middle.start()

    def edge(valid, source, target, sem):
        @pl.when(valid)
        def _():
            copy = pltpu.make_async_copy(
                wave.at[:, :, pl.ds(pl.multiple_of(source, MR), MR)], window.at[:, :, pl.ds(target, MR)], sem
            )
            copy.start()
            copy.wait()

        @pl.when(jnp.logical_not(valid))
        def _():
            window[:, :, pl.ds(target, MR)] = jnp.zeros((VECS, ML, MR), jnp.bfloat16)

    edge(op > 0, start - MR, 0, sems.at[1])
    edge(op < n_op - 1, start + width, MR + width, sems.at[2])
    middle.wait()


def window_of(wave, n_op):
    width = wave.shape[2] // n_op
    return pl.pallas_call(
        functools.partial(window_kernel, n_op),
        out_shape=in_vmem((VECS, ML, width + 2 * MR)),
        in_specs=[HBM],
        out_specs=VMEM,
        scratch_shapes=[pltpu.SemaphoreType.DMA((3,))],
        compiler_params=grant(4),
        cost_estimate=cost(0, 2 * 1024 * 1024),
        name="window",
    )(in_hbm(wave))


def left_kernel(*refs):
    *lefts, window, z_ref = refs
    per = z_ref.shape[0]
    width = per * MR
    terms = lefts[0].shape[0] // ML
    for piece, left in enumerate(lefts):
        for inner in range(terms):
            term = piece * terms + inner
            offset = pl.multiple_of((1 + shift_of(left, inner)) * MR, MR)
            for v in range(VECS):
                z = jnp.dot(
                    left[inner * ML : (inner + 1) * ML], window[v, :, pl.ds(offset, width)], preferred_element_type=jnp.float32
                ).astype(jnp.bfloat16)
                for column in range(per):
                    z_ref[column, v, :, term * MR : (term + 1) * MR] = z[:, column * MR : (column + 1) * MR]


def left_products(lefts, window):
    terms = len(lefts) * (lefts[0].shape[0] // ML)
    width = window.shape[2] - 2 * MR
    return pl.pallas_call(
        left_kernel,
        out_shape=in_vmem((width // MR, VECS, ML, terms * MR)),
        in_specs=[VMEM] * (len(lefts) + 1),
        out_specs=VMEM,
        compiler_params=grant(8 + 4 * width // MR),
        cost_estimate=cost(2 * terms * VECS * ML * ML * width, 1024 * 1024),
        name="left_products",
    )(*lefts, window)


def right_kernel(cls, per, z_ref, own, other, received, *refs):
    *lefts, zero_ref, low_ref, high_ref, total = refs
    sec = lax.axis_index("sec")
    column = (sec % per) ^ cls
    even = sec % 2 == 0
    settled = on_own_side(per, 1)
    half, terms = own.shape[0], own.shape[1]
    total[...] = jnp.zeros_like(total)
    for piece, left in enumerate(lefts):
        for inner in range(terms):
            term = piece * terms + inner
            kind = 1 + shift_of(left, inner)
            if piece < half:
                block = jnp.where(settled, own[piece, inner], other[piece, inner])
            else:
                block = received[piece - half, inner]
            for v in range(VECS):
                total[kind, v] += jnp.dot(
                    z_ref[column, v, :, term * MR : (term + 1) * MR], block, preferred_element_type=jnp.float32
                )
    for v in range(VECS):
        down, up = total[0, v].astype(jnp.bfloat16), total[2, v].astype(jnp.bfloat16)
        zero_ref[v] = total[1, v]
        low_ref[v] = jnp.where(even, up, down)
        high_ref[v] = jnp.where(even, down, up)


def right_products(cls, per, z, own, other, received, lefts):
    block = (VECS, ML, MR)
    return pl.pallas_call(
        functools.partial(right_kernel, cls, per),
        out_shape=[jax.ShapeDtypeStruct(block, dtype) for dtype in (jnp.float32, jnp.bfloat16, jnp.bfloat16)],
        in_specs=[VMEM] * (4 + len(lefts)),
        out_specs=[VMEM] * 3,
        scratch_shapes=[in_vmem((3,) + block, jnp.float32)],
        compiler_params=grant(8),
        cost_estimate=cost(0, 0),
        name="right_products",
    )(z, own, other, received, *lefts)


def sum_kernel(per, *refs):
    *parts, out_hbm, out_ref, sems = refs
    zeros, lows, highs = parts[::3], parts[1::3], parts[2::3]
    sec = lax.axis_index("sec")
    beyond = (sec ^ ((((sec + 1) ^ 1) + per - 1) % per)) % per
    copies = [pltpu.make_async_copy(out_ref.at[v], out_hbm.at[v], sems.at[v]) for v in range(VECS)]

    def add(high):
        @pl.when(beyond == high)
        def _():
            for v in range(VECS):
                for cls in range(per):
                    column = pl.multiple_of(((sec % per) ^ cls) * MR, MR)
                    total = zeros[cls][v].astype(jnp.float32) + lows[cls ^ 1][v].astype(jnp.float32)
                    total = total + highs[cls ^ high][v].astype(jnp.float32)
                    out_ref[v, :, pl.ds(column, MR)] = total.astype(jnp.bfloat16)
                copies[v].start()

    carry = 1
    while carry < per:
        add(carry)
        carry = 2 * carry + 1
    for copy in copies:
        copy.wait()


def summed(per, parts):
    shape = (VECS, ML, per * MR)
    return pl.pallas_call(
        functools.partial(sum_kernel, per),
        out_shape=jax.ShapeDtypeStruct(shape, jnp.bfloat16),
        in_specs=[VMEM] * len(parts),
        out_specs=HBM,
        scratch_shapes=[in_vmem(shape), pltpu.SemaphoreType.DMA((VECS,))],
        compiler_params=grant(8),
        name="summed",
    )(*parts)


def on_device(n_op, n_sec, wavefunction, left_ops, right_ops, term_shift):
    per = n_sec // n_op
    tie = lax.optimization_barrier
    matching = lax.axis_index("op") ^ (lax.axis_index("sec") // per)
    held = right_ops.reshape((1,) + right_ops.shape[:1] + right_ops.shape[2:])
    packed, kept = pack(term_shift, left_ops.transpose(1, 0, 2).reshape(-1, ML), held)
    window = window_of(wavefunction.transpose(1, 0, 2), n_op)
    lefts = [packed]
    bit = n_op // 2
    while bit > 1:
        one, two, window = tie((*towards_owner(held, n_op, n_sec, bit), window))
        same = (matching & bit) == 0
        held = kept = jnp.concatenate([jnp.where(same, kept, one), jnp.where(same, one, two)])
        lefts = lefts + [over_op(x, n_op, bit) for x in lefts]
        bit //= 2
    lefts = lefts + [over_op(x, n_op, 1) for x in lefts]
    owns = [held]
    bit = 1
    while bit < per:
        owns = owns + [over_sec(c, n_sec, bit) for c in owns]
        bit *= 2
    other, owns = tie((over_sec(owns[0], n_sec, per), owns))
    z = left_products(lefts, window)
    low = [(d, d ^ 1) for d in range(n_sec)]
    high = [(d, ((d + 1) ^ 1) - 1) for d in range(1, n_sec - 1)]
    settled = (matching & 1) == 0
    parts, others = [], [other]
    for cls, own in enumerate(owns):
        received = over_op(jnp.where(settled, other, own), n_op, 1)
        later = None
        if cls + 1 < per:
            half = own.shape[0] // 2
            step = (cls + 1) & -(cls + 1)
            later = [
                over_sec(owns[cls + 1][:half], n_sec, per),
                over_sec(others[(cls + 1) ^ step][half:], n_sec, step),
            ]
        zero, to_low, to_high = right_products(cls, per, z, own, other, received, lefts)
        parts += [zero, lax.ppermute(to_low, "sec", low), lax.ppermute(to_high, "sec", high)]
        if later is not None:
            later, parts[-3] = tie((later, zero.astype(jnp.bfloat16)))
            other = jnp.concatenate(later)
            others.append(other)
    return summed(per, parts).transpose(1, 0, 2)


def solution(mesh):
    in_specs = (P("sec", None, None), P("sec", "op", None), P("op", "sec", None, None), P("op"))
    out_specs = P("sec", None, "op")
    return jax.shard_map(
        functools.partial(on_device, mesh.shape["op"], mesh.shape["sec"]),
        mesh=mesh,
        in_specs=in_specs,
        out_specs=out_specs,
        check_vma=False,
    )
```

```python
import functools

import jax
import jax.numpy as jnp
from jax import lax
from jax.experimental import pallas as pl
from jax.experimental.pallas import tpu as pltpu
from jax.sharding import PartitionSpec as P

ML = 256
MR = 128
VECS = 3
TILE = 16
VMEM = pl.BlockSpec(memory_space=pltpu.VMEM)
HBM = pl.BlockSpec(memory_space=pltpu.HBM)


def in_vmem(shape, dtype=jnp.bfloat16):
    return pltpu.VMEM(shape, dtype)


def in_hbm(x):
    return pltpu.with_memory_space_constraint(x, pltpu.HBM)


def grant(mebibytes):
    return pltpu.CompilerParams(vmem_limit_bytes=mebibytes * 1024 * 1024)


def cost(flops, bytes_accessed):
    return pl.CostEstimate(flops=flops, bytes_accessed=bytes_accessed, transcendentals=0)


def over_op(x, n_op, bit):
    return lax.ppermute(x, "op", [(o, o ^ bit) for o in range(n_op)])


def over_sec(x, n_sec, bit):
    return lax.ppermute(x, "sec", [(d, d ^ bit) for d in range(n_sec)])


def on_own_side(per, bit):
    return ((lax.axis_index("op") ^ (lax.axis_index("sec") // per)) & bit) == 0


def towards_owner(held, n_op, n_sec, bit):
    per = n_sec // n_op
    first, second = [], []
    for o in range(n_op):
        for d in range(n_sec):
            source = o * n_sec + d
            far = d ^ (bit * per)
            if (o & bit) == ((d // per) & bit):
                first.append((source, o * n_sec + far))
            else:
                first.append((source, (o ^ bit) * n_sec + d))
                second.append((source, (o ^ bit) * n_sec + far))
    return lax.ppermute(held, ("op", "sec"), first), lax.ppermute(held, ("op", "sec"), second)


def route_kernel(per, bit, held, one, two, out_ref):
    half = held.shape[0]
    own = on_own_side(per, bit)
    out_ref[:half] = jnp.where(own, held[...], one[...])
    out_ref[half:] = jnp.where(own, one[...], two[...])


def route(held, one, two, per, bit):
    return pl.pallas_call(
        functools.partial(route_kernel, per, bit),
        out_shape=in_vmem((2 * held.shape[0],) + held.shape[1:]),
        in_specs=[VMEM] * 3,
        out_specs=VMEM,
        compiler_params=grant(4),
        cost_estimate=cost(0, 0),
        name="route",
    )(held, one, two)


def pick_kernel(per, own, other, out_ref):
    out_ref[...] = jnp.where(on_own_side(per, 1), other[...], own[...])


def pick(own, other, per):
    return pl.pallas_call(
        functools.partial(pick_kernel, per),
        out_shape=in_vmem(own.shape),
        in_specs=[VMEM] * 2,
        out_specs=VMEM,
        compiler_params=grant(4),
        cost_estimate=cost(0, 0),
        name="pick",
    )(own, other)


def shift_of(left, inner):
    row = left.shape[0] - TILE + inner
    return jnp.max(left[row : row + 1, :MR].astype(jnp.float32)).astype(jnp.int32)


def pack_kernel(shift, left, right, packed, kept, shift_ref, sems):
    rows = left.shape[0]
    copies = [
        pltpu.make_async_copy(shift, shift_ref, sems.at[0]),
        pltpu.make_async_copy(left, packed.at[pl.ds(0, rows)], sems.at[1]),
        pltpu.make_async_copy(right, kept, sems.at[2]),
    ]
    for copy in copies:
        copy.start()
    copies[0].wait()
    row = lax.broadcasted_iota(jnp.int32, (TILE, ML), 0)
    tags = jnp.zeros((TILE, ML), jnp.float32)
    for inner in range(rows // ML):
        tags = jnp.where(row == inner, shift_ref[inner].astype(jnp.float32), tags)
    packed[rows:] = tags.astype(jnp.bfloat16)
    for copy in copies[1:]:
        copy.wait()


def pack(shift, left, right):
    return pl.pallas_call(
        pack_kernel,
        out_shape=[in_vmem((left.shape[0] + TILE, ML)), in_vmem(right.shape)],
        in_specs=[HBM] * 3,
        out_specs=[VMEM] * 2,
        scratch_shapes=[pltpu.SMEM(shift.shape, jnp.int32), pltpu.SemaphoreType.DMA((3,))],
        compiler_params=grant(8),
        cost_estimate=cost(0, 32 * 1024 * 1024),
        name="pack",
    )(in_hbm(shift), in_hbm(left), in_hbm(right))


def window_kernel(n_op, wave, window, sems):
    width = window.shape[2] - 2 * MR
    op = lax.axis_index("op")
    start = pl.multiple_of(op * width, MR)
    middle = pltpu.make_async_copy(
        wave.at[:, :, pl.ds(start, width)], window.at[:, :, pl.ds(MR, width)], sems.at[0]
    )
    middle.start()

    def edge(valid, source, target, sem):
        @pl.when(valid)
        def _():
            copy = pltpu.make_async_copy(
                wave.at[:, :, pl.ds(pl.multiple_of(source, MR), MR)], window.at[:, :, pl.ds(target, MR)], sem
            )
            copy.start()
            copy.wait()

        @pl.when(jnp.logical_not(valid))
        def _():
            window[:, :, pl.ds(target, MR)] = jnp.zeros((VECS, ML, MR), jnp.bfloat16)

    edge(op > 0, start - MR, 0, sems.at[1])
    edge(op < n_op - 1, start + width, MR + width, sems.at[2])
    middle.wait()


def window_of(wave, n_op):
    width = wave.shape[2] // n_op
    return pl.pallas_call(
        functools.partial(window_kernel, n_op),
        out_shape=in_vmem((VECS, ML, width + 2 * MR)),
        in_specs=[HBM],
        out_specs=VMEM,
        scratch_shapes=[pltpu.SemaphoreType.DMA((3,))],
        compiler_params=grant(4),
        cost_estimate=cost(0, 2 * 1024 * 1024),
        name="window",
    )(in_hbm(wave))


def left_kernel(*refs):
    *lefts, window, z_ref = refs
    per = z_ref.shape[0]
    width = per * MR
    terms = lefts[0].shape[0] // ML
    for piece, left in enumerate(lefts):
        for inner in range(terms):
            term = piece * terms + inner
            offset = pl.multiple_of((1 + shift_of(left, inner)) * MR, MR)
            for v in range(VECS):
                z = jnp.dot(
                    left[inner * ML : (inner + 1) * ML], window[v, :, pl.ds(offset, width)], preferred_element_type=jnp.float32
                ).astype(jnp.bfloat16)
                for column in range(per):
                    z_ref[column, v, :, term * MR : (term + 1) * MR] = z[:, column * MR : (column + 1) * MR]


def left_products(lefts, window):
    terms = len(lefts) * (lefts[0].shape[0] // ML)
    width = window.shape[2] - 2 * MR
    return pl.pallas_call(
        left_kernel,
        out_shape=in_vmem((width // MR, VECS, ML, terms * MR)),
        in_specs=[VMEM] * (len(lefts) + 1),
        out_specs=VMEM,
        compiler_params=grant(8 + 4 * width // MR),
        cost_estimate=cost(2 * terms * VECS * ML * ML * width, 1024 * 1024),
        name="left_products",
    )(*lefts, window)


def right_kernel(cls, per, z_ref, own, other, received, *refs):
    *lefts, zero_ref, low_ref, high_ref, total = refs
    sec = lax.axis_index("sec")
    column = (sec % per) ^ cls
    even = sec % 2 == 0
    settled = on_own_side(per, 1)
    half, terms = own.shape[0], own.shape[1]
    total[...] = jnp.zeros_like(total)
    for piece, left in enumerate(lefts):
        for inner in range(terms):
            term = piece * terms + inner
            kind = 1 + shift_of(left, inner)
            if piece < half:
                block = jnp.where(settled, own[piece, inner], other[piece, inner])
            else:
                block = received[piece - half, inner]
            for v in range(VECS):
                total[kind, v] += jnp.dot(
                    z_ref[column, v, :, term * MR : (term + 1) * MR], block, preferred_element_type=jnp.float32
                )
    for v in range(VECS):
        down, up = total[0, v], total[2, v]
        zero_ref[v] = total[1, v]
        low_ref[v] = jnp.where(even, up, down).astype(low_ref.dtype)
        high_ref[v] = jnp.where(even, down, up).astype(high_ref.dtype)


def right_products(cls, per, through, z, own, other, received, lefts):
    block = (VECS, ML, MR)
    low_type = jnp.float32 if through else jnp.bfloat16
    return pl.pallas_call(
        functools.partial(right_kernel, cls, per),
        out_shape=[jax.ShapeDtypeStruct(block, dtype) for dtype in (jnp.float32, low_type, jnp.bfloat16)],
        in_specs=[VMEM] * (4 + len(lefts)),
        out_specs=[VMEM] * 3,
        scratch_shapes=[in_vmem((3,) + block, jnp.float32)],
        compiler_params=grant(8),
        cost_estimate=cost(0, 0),
        name="right_products",
    )(z, own, other, received, *lefts)


def joined_kernel(low, passing, out_ref):
    out_ref[...] = (low[...] + passing[...].astype(jnp.float32)).astype(jnp.bfloat16)


def joined(low, passing):
    return pl.pallas_call(
        joined_kernel,
        out_shape=jax.ShapeDtypeStruct(low.shape, jnp.bfloat16),
        in_specs=[VMEM] * 2,
        out_specs=VMEM,
        compiler_params=grant(8),
        cost_estimate=cost(0, 0),
        name="joined",
    )(low, passing)


def sum_kernel(per, direct, *refs):
    *parts, out_hbm, out_ref, sems = refs
    zeros, lows, highs = parts[:per], parts[per : 2 * per], dict(zip(direct, parts[2 * per :]))
    sec = lax.axis_index("sec")
    beyond = (sec ^ ((((sec + 1) ^ 1) + per - 1) % per)) % per
    copies = [pltpu.make_async_copy(out_ref.at[v], out_hbm.at[v], sems.at[v]) for v in range(VECS)]

    def add(high):
        @pl.when(beyond == high)
        def _():
            for v in range(VECS):
                for cls in range(per):
                    column = pl.multiple_of(((sec % per) ^ cls) * MR, MR)
                    total = zeros[cls][v].astype(jnp.float32) + lows[cls ^ 1][v].astype(jnp.float32)
                    if cls ^ high in highs:
                        total = total + highs[cls ^ high][v].astype(jnp.float32)
                    out_ref[v, :, pl.ds(column, MR)] = total.astype(jnp.bfloat16)
                copies[v].start()

    carry = 1
    while carry < per:
        add(carry)
        carry = 2 * carry + 1
    for copy in copies:
        copy.wait()


def summed(per, direct, parts):
    shape = (VECS, ML, per * MR)
    return pl.pallas_call(
        functools.partial(sum_kernel, per, direct),
        out_shape=jax.ShapeDtypeStruct(shape, jnp.bfloat16),
        in_specs=[VMEM] * len(parts),
        out_specs=HBM,
        scratch_shapes=[in_vmem(shape), pltpu.SemaphoreType.DMA((VECS,))],
        compiler_params=grant(8),
        name="summed",
    )(*parts)


def on_device(n_op, n_sec, wavefunction, left_ops, right_ops, term_shift):
    per = n_sec // n_op
    tie = lax.optimization_barrier
    matching = lax.axis_index("op") ^ (lax.axis_index("sec") // per)
    held = right_ops.reshape((1,) + right_ops.shape[:1] + right_ops.shape[2:])
    packed, kept = pack(term_shift, left_ops.transpose(1, 0, 2).reshape(-1, ML), held)
    window = window_of(wavefunction.transpose(1, 0, 2), n_op)
    lefts = [packed]
    bit = n_op // 2
    while bit > 1:
        one, two, window = tie((*towards_owner(held, n_op, n_sec, bit), window))
        same = (matching & bit) == 0
        held = kept = jnp.concatenate([jnp.where(same, kept, one), jnp.where(same, one, two)])
        lefts = lefts + [over_op(x, n_op, bit) for x in lefts]
        bit //= 2
    lefts = lefts + [over_op(x, n_op, 1) for x in lefts]
    owns = [held]
    bit = 1
    while bit < per:
        owns = owns + [over_sec(c, n_sec, bit) for c in owns]
        bit *= 2
    other, owns = tie((over_sec(owns[0], n_sec, per), owns))
    z = left_products(lefts, window)
    low = [(d, d ^ 1) for d in range(n_sec)]
    high = [(d, ((d + 1) ^ 1) - 1) for d in range(1, n_sec - 1)]
    through = (0,)
    along = [(d, d + 2 if d % 2 else d - 2) for d in range(1, n_sec - 1)]
    settled = (matching & 1) == 0
    parts, others = [], [other]
    for cls, own in enumerate(owns):
        received = over_op(jnp.where(settled, other, own), n_op, 1)
        later = None
        if cls + 1 < per:
            half = own.shape[0] // 2
            step = (cls + 1) & -(cls + 1)
            later = [
                over_sec(owns[cls + 1][:half], n_sec, per),
                over_sec(others[(cls + 1) ^ step][half:], n_sec, step),
            ]
        zero, to_low, to_high = right_products(cls, per, cls in through, z, own, other, received, lefts)
        if cls in through:
            passing = lax.ppermute(to_high, "sec", along)
            parts += [zero, to_low, passing]
        else:
            parts += [zero, lax.ppermute(to_low, "sec", low), lax.ppermute(to_high, "sec", high)]
        if later is not None:
            later, parts[-3] = tie((later, zero.astype(jnp.bfloat16)))
            other = jnp.concatenate(later)
            others.append(other)
    parts[1] = lax.ppermute(joined(tie((parts[1], parts[3]))[0], parts[2]), "sec", low)
    direct = [cls for cls in range(per) if cls not in through]
    parts = parts[::3] + parts[1::3] + [parts[3 * cls + 2] for cls in direct]
    return summed(per, direct, parts).transpose(1, 0, 2)


def solution(mesh):
    in_specs = (P("sec", None, None), P("sec", "op", None), P("op", "sec", None, None), P("op"))
    out_specs = P("sec", None, "op")
    return jax.shard_map(
        functools.partial(on_device, mesh.shape["op"], mesh.shape["sec"]),
        mesh=mesh,
        in_specs=in_specs,
        out_specs=out_specs,
        check_vma=False,
    )
```

```python
import functools

import jax
import jax.numpy as jnp
from jax import lax
from jax.experimental import pallas as pl
from jax.experimental.pallas import tpu as pltpu
from jax.sharding import PartitionSpec as P

ML = 256
MR = 128
VECS = 3
TILE = 16
VMEM = pl.BlockSpec(memory_space=pltpu.VMEM)
HBM = pl.BlockSpec(memory_space=pltpu.HBM)


def in_vmem(shape, dtype=jnp.bfloat16):
    return pltpu.VMEM(shape, dtype)


def in_hbm(x):
    return pltpu.with_memory_space_constraint(x, pltpu.HBM)


def grant(mebibytes):
    return pltpu.CompilerParams(vmem_limit_bytes=mebibytes * 1024 * 1024)


def cost(flops, bytes_accessed):
    return pl.CostEstimate(flops=flops, bytes_accessed=bytes_accessed, transcendentals=0)


def over_op(x, n_op, bit):
    return lax.ppermute(x, "op", [(o, o ^ bit) for o in range(n_op)])


def over_sec(x, n_sec, bit):
    return lax.ppermute(x, "sec", [(d, d ^ bit) for d in range(n_sec)])


def on_own_side(per, bit):
    return ((lax.axis_index("op") ^ (lax.axis_index("sec") // per)) & bit) == 0


def towards_owner(held, n_op, n_sec, bit):
    per = n_sec // n_op
    first, second = [], []
    for o in range(n_op):
        for d in range(n_sec):
            source = o * n_sec + d
            far = d ^ (bit * per)
            if (o & bit) == ((d // per) & bit):
                first.append((source, o * n_sec + far))
            else:
                first.append((source, (o ^ bit) * n_sec + d))
                second.append((source, (o ^ bit) * n_sec + far))
    return lax.ppermute(held, ("op", "sec"), first), lax.ppermute(held, ("op", "sec"), second)


def route_kernel(per, bit, held, one, two, out_ref):
    half = held.shape[0]
    own = on_own_side(per, bit)
    out_ref[:half] = jnp.where(own, held[...], one[...])
    out_ref[half:] = jnp.where(own, one[...], two[...])


def route(held, one, two, per, bit):
    return pl.pallas_call(
        functools.partial(route_kernel, per, bit),
        out_shape=in_vmem((2 * held.shape[0],) + held.shape[1:]),
        in_specs=[VMEM] * 3,
        out_specs=VMEM,
        compiler_params=grant(4),
        cost_estimate=cost(0, 0),
        name="route",
    )(held, one, two)


def pick_kernel(per, own, other, out_ref):
    out_ref[...] = jnp.where(on_own_side(per, 1), other[...], own[...])


def pick(own, other, per):
    return pl.pallas_call(
        functools.partial(pick_kernel, per),
        out_shape=in_vmem(own.shape),
        in_specs=[VMEM] * 2,
        out_specs=VMEM,
        compiler_params=grant(4),
        cost_estimate=cost(0, 0),
        name="pick",
    )(own, other)


def shift_of(left, inner):
    tags = left[left.shape[0] - TILE :, :MR].astype(jnp.float32)
    row = lax.broadcasted_iota(jnp.int32, tags.shape, 0)
    return jnp.max(jnp.where(row == inner, tags, -1.0)).astype(jnp.int32)


def pack_kernel(shift, left, right, packed, kept, shift_ref, sems):
    rows = left.shape[0]
    copies = [
        pltpu.make_async_copy(shift, shift_ref, sems.at[0]),
        pltpu.make_async_copy(left, packed.at[pl.ds(0, rows)], sems.at[1]),
        pltpu.make_async_copy(right, kept, sems.at[2]),
    ]
    for copy in copies:
        copy.start()
    copies[0].wait()
    row = lax.broadcasted_iota(jnp.int32, (TILE, ML), 0)
    tags = jnp.zeros((TILE, ML), jnp.float32)
    for inner in range(rows // ML):
        tags = jnp.where(row == inner, shift_ref[inner].astype(jnp.float32), tags)
    packed[rows:] = tags.astype(jnp.bfloat16)
    for copy in copies[1:]:
        copy.wait()


def pack(shift, left, right):
    return pl.pallas_call(
        pack_kernel,
        out_shape=[in_vmem((left.shape[0] + TILE, ML)), in_vmem(right.shape)],
        in_specs=[HBM] * 3,
        out_specs=[VMEM] * 2,
        scratch_shapes=[pltpu.SMEM(shift.shape, jnp.int32), pltpu.SemaphoreType.DMA((3,))],
        compiler_params=grant(8),
        cost_estimate=cost(0, 32 * 1024 * 1024),
        name="pack",
    )(in_hbm(shift), in_hbm(left), in_hbm(right))


def window_kernel(n_op, wave, window, sems):
    width = window.shape[2] - 2 * MR
    op = lax.axis_index("op")
    start = pl.multiple_of(op * width, MR)
    middle = pltpu.make_async_copy(
        wave.at[:, :, pl.ds(start, width)], window.at[:, :, pl.ds(MR, width)], sems.at[0]
    )
    middle.start()

    def edge(valid, source, target, sem):
        @pl.when(valid)
        def _():
            copy = pltpu.make_async_copy(
                wave.at[:, :, pl.ds(pl.multiple_of(source, MR), MR)], window.at[:, :, pl.ds(target, MR)], sem
            )
            copy.start()
            copy.wait()

        @pl.when(jnp.logical_not(valid))
        def _():
            window[:, :, pl.ds(target, MR)] = jnp.zeros((VECS, ML, MR), jnp.bfloat16)

    edge(op > 0, start - MR, 0, sems.at[1])
    edge(op < n_op - 1, start + width, MR + width, sems.at[2])
    middle.wait()


def window_of(wave, n_op):
    width = wave.shape[2] // n_op
    return pl.pallas_call(
        functools.partial(window_kernel, n_op),
        out_shape=in_vmem((VECS, ML, width + 2 * MR)),
        in_specs=[HBM],
        out_specs=VMEM,
        scratch_shapes=[pltpu.SemaphoreType.DMA((3,))],
        compiler_params=grant(4),
        cost_estimate=cost(0, 2 * 1024 * 1024),
        name="window",
    )(in_hbm(wave))


def left_kernel(*refs):
    *lefts, window, z_ref = refs
    per = z_ref.shape[0]
    width = per * MR
    terms = lefts[0].shape[0] // ML
    for piece, left in enumerate(lefts):
        for inner in range(terms):
            term = piece * terms + inner
            offset = pl.multiple_of((1 + shift_of(left, inner)) * MR, MR)
            for v in range(VECS):
                z = jnp.dot(
                    left[inner * ML : (inner + 1) * ML], window[v, :, pl.ds(offset, width)], preferred_element_type=jnp.float32
                ).astype(jnp.bfloat16)
                for column in range(per):
                    z_ref[column, v, :, term * MR : (term + 1) * MR] = z[:, column * MR : (column + 1) * MR]


def left_products(lefts, window):
    terms = len(lefts) * (lefts[0].shape[0] // ML)
    width = window.shape[2] - 2 * MR
    return pl.pallas_call(
        left_kernel,
        out_shape=in_vmem((width // MR, VECS, ML, terms * MR)),
        in_specs=[VMEM] * (len(lefts) + 1),
        out_specs=VMEM,
        compiler_params=grant(8 + 4 * width // MR),
        cost_estimate=cost(2 * terms * VECS * ML * ML * width, 1024 * 1024),
        name="left_products",
    )(*lefts, window)


def right_kernel(cls, per, z_ref, own, other, received, *refs):
    *lefts, zero_ref, low_ref, high_ref, total = refs
    sec = lax.axis_index("sec")
    column = (sec % per) ^ cls
    even = sec % 2 == 0
    settled = on_own_side(per, 1)
    half, terms = own.shape[0], own.shape[1]
    total[...] = jnp.zeros_like(total)
    for piece, left in enumerate(lefts):
        for inner in range(terms):
            term = piece * terms + inner
            kind = 1 + shift_of(left, inner)
            if piece < half:
                block = jnp.where(settled, own[piece, inner], other[piece, inner])
            else:
                block = received[piece - half, inner]
            for v in range(VECS):
                total[kind, v] += jnp.dot(
                    z_ref[column, v, :, term * MR : (term + 1) * MR], block, preferred_element_type=jnp.float32
                )
    for v in range(VECS):
        down, up = total[0, v], total[2, v]
        zero_ref[v] = total[1, v]
        low_ref[v] = jnp.where(even, up, down).astype(low_ref.dtype)
        high_ref[v] = jnp.where(even, down, up).astype(high_ref.dtype)


def right_products(cls, per, through, z, own, other, received, lefts):
    block = (VECS, ML, MR)
    low_type = jnp.float32 if through else jnp.bfloat16
    return pl.pallas_call(
        functools.partial(right_kernel, cls, per),
        out_shape=[jax.ShapeDtypeStruct(block, dtype) for dtype in (jnp.float32, low_type, jnp.bfloat16)],
        in_specs=[VMEM] * (4 + len(lefts)),
        out_specs=[VMEM] * 3,
        scratch_shapes=[in_vmem((3,) + block, jnp.float32)],
        compiler_params=grant(8),
        cost_estimate=cost(0, 0),
        name="right_products",
    )(z, own, other, received, *lefts)


def joined_kernel(low, passing, out_ref):
    out_ref[...] = (low[...] + passing[...].astype(jnp.float32)).astype(jnp.bfloat16)


def joined(low, passing):
    return pl.pallas_call(
        joined_kernel,
        out_shape=jax.ShapeDtypeStruct(low.shape, jnp.bfloat16),
        in_specs=[VMEM] * 2,
        out_specs=VMEM,
        compiler_params=grant(8),
        cost_estimate=cost(0, 0),
        name="joined",
    )(low, passing)


def sum_kernel(per, direct, *refs):
    *parts, out_hbm, out_ref, sems = refs
    zeros, lows, highs = parts[:per], parts[per : 2 * per], dict(zip(direct, parts[2 * per :]))
    sec = lax.axis_index("sec")
    beyond = (sec ^ ((((sec + 1) ^ 1) + per - 1) % per)) % per
    copies = [pltpu.make_async_copy(out_ref.at[v], out_hbm.at[v], sems.at[v]) for v in range(VECS)]

    def add(high):
        @pl.when(beyond == high)
        def _():
            for v in range(VECS):
                for cls in range(per):
                    column = pl.multiple_of(((sec % per) ^ cls) * MR, MR)
                    total = zeros[cls][v].astype(jnp.float32) + lows[cls ^ 1][v].astype(jnp.float32)
                    if cls ^ high in highs:
                        total = total + highs[cls ^ high][v].astype(jnp.float32)
                    out_ref[v, :, pl.ds(column, MR)] = total.astype(jnp.bfloat16)
                copies[v].start()
            for copy in copies:
                copy.wait()

    carry = 1
    while carry < per:
        add(carry)
        carry = 2 * carry + 1


def summed(per, direct, parts):
    shape = (VECS, ML, per * MR)
    return pl.pallas_call(
        functools.partial(sum_kernel, per, direct),
        out_shape=jax.ShapeDtypeStruct(shape, jnp.bfloat16),
        in_specs=[VMEM] * len(parts),
        out_specs=HBM,
        scratch_shapes=[in_vmem(shape), pltpu.SemaphoreType.DMA((VECS,))],
        compiler_params=grant(8),
        name="summed",
    )(*parts)


def on_device(n_op, n_sec, wavefunction, left_ops, right_ops, term_shift):
    per = n_sec // n_op
    tie = lax.optimization_barrier
    matching = lax.axis_index("op") ^ (lax.axis_index("sec") // per)
    held = right_ops.reshape((1,) + right_ops.shape[:1] + right_ops.shape[2:])
    packed, kept = pack(term_shift, left_ops.transpose(1, 0, 2).reshape(-1, ML), held)
    window = window_of(wavefunction.transpose(1, 0, 2), n_op)
    lefts = [packed]
    bit = n_op // 2
    while bit > 1:
        one, two, window = tie((*towards_owner(held, n_op, n_sec, bit), window))
        same = (matching & bit) == 0
        held = kept = jnp.concatenate([jnp.where(same, kept, one), jnp.where(same, one, two)])
        lefts = lefts + [over_op(x, n_op, bit) for x in lefts]
        bit //= 2
    lefts = lefts + [over_op(x, n_op, 1) for x in lefts]
    owns = [held]
    bit = 1
    while bit < per:
        owns = owns + [over_sec(c, n_sec, bit) for c in owns]
        bit *= 2
    other, owns = tie((over_sec(owns[0], n_sec, per), owns))
    z = left_products(lefts, window)
    low = [(d, d ^ 1) for d in range(n_sec)]
    high = [(d, ((d + 1) ^ 1) - 1) for d in range(1, n_sec - 1)]
    turn = 2 % per
    through = sorted({0, turn}) if per <= 4 else []
    lows = []
    along = [(d, d + 2 if d % 2 else d - 2) for d in range(1, n_sec - 1)]
    settled = (matching & 1) == 0
    parts, others = [], [other]
    for cls, own in enumerate(owns):
        received = over_op(jnp.where(settled, other, own), n_op, 1)
        later = None
        if cls + 1 < per:
            half = own.shape[0] // 2
            step = (cls + 1) & -(cls + 1)
            later = [
                over_sec(owns[cls + 1][:half], n_sec, per),
                over_sec(others[(cls + 1) ^ step][half:], n_sec, step),
            ]
        zero, to_low, to_high = right_products(cls, per, cls in through, z, own, other, received, lefts)
        if cls in through:
            passing = lax.ppermute(to_high, "sec", along)
            parts += [zero, to_low, passing]
        else:
            parts += [zero, lax.ppermute(to_low, "sec", low), lax.ppermute(to_high, "sec", high)]
        if later is not None:
            later, parts[-3] = tie((later, zero.astype(jnp.bfloat16)))
            other = jnp.concatenate(later)
            others.append(other)
    for cls in through:
        own_low = tie((parts[3 * cls + 1], parts[3]))[0]
        lows.append(lax.ppermute(joined(own_low, parts[3 * (cls ^ turn) + 2]), "sec", low))
    for cls, part in zip(through, lows):
        parts[3 * cls + 1] = part
    direct = [cls for cls in range(per) if cls not in through]
    parts = parts[::3] + parts[1::3] + [parts[3 * cls + 2] for cls in direct]
    return summed(per, direct, parts).transpose(1, 0, 2)


def solution(mesh):
    in_specs = (P("sec", None, None), P("sec", "op", None), P("op", "sec", None, None), P("op"))
    out_specs = P("sec", None, "op")
    return jax.shard_map(
        functools.partial(on_device, mesh.shape["op"], mesh.shape["sec"]),
        mesh=mesh,
        in_specs=in_specs,
        out_specs=out_specs,
        check_vma=False,
    )
```

```python
import functools

import jax
import jax.numpy as jnp
from jax import lax
from jax.experimental import pallas as pl
from jax.experimental.pallas import tpu as pltpu
from jax.sharding import PartitionSpec as P

ML = 256
MR = 128
VECS = 3
TILE = 16
VMEM = pl.BlockSpec(memory_space=pltpu.VMEM)
HBM = pl.BlockSpec(memory_space=pltpu.HBM)


def in_vmem(shape, dtype=jnp.bfloat16):
    return pltpu.VMEM(shape, dtype)


def in_hbm(x):
    return pltpu.with_memory_space_constraint(x, pltpu.HBM)


def grant(mebibytes):
    return pltpu.CompilerParams(vmem_limit_bytes=mebibytes * 1024 * 1024)


def cost(flops, bytes_accessed):
    return pl.CostEstimate(flops=flops, bytes_accessed=bytes_accessed, transcendentals=0)


def over_op(x, n_op, bit):
    return lax.ppermute(x, "op", [(o, o ^ bit) for o in range(n_op)])


def over_sec(x, n_sec, bit):
    return lax.ppermute(x, "sec", [(d, d ^ bit) for d in range(n_sec)])


def on_own_side(per, bit):
    return ((lax.axis_index("op") ^ (lax.axis_index("sec") // per)) & bit) == 0


def towards_owner(held, n_op, n_sec, bit):
    per = n_sec // n_op
    first, second = [], []
    for o in range(n_op):
        for d in range(n_sec):
            source = o * n_sec + d
            far = d ^ (bit * per)
            if (o & bit) == ((d // per) & bit):
                first.append((source, o * n_sec + far))
            else:
                first.append((source, (o ^ bit) * n_sec + d))
                second.append((source, (o ^ bit) * n_sec + far))
    return lax.ppermute(held, ("op", "sec"), first), lax.ppermute(held, ("op", "sec"), second)


def route_kernel(per, bit, held, one, two, out_ref):
    half = held.shape[0]
    own = on_own_side(per, bit)
    out_ref[:half] = jnp.where(own, held[...], one[...])
    out_ref[half:] = jnp.where(own, one[...], two[...])


def route(held, one, two, per, bit):
    return pl.pallas_call(
        functools.partial(route_kernel, per, bit),
        out_shape=in_vmem((2 * held.shape[0],) + held.shape[1:]),
        in_specs=[VMEM] * 3,
        out_specs=VMEM,
        compiler_params=grant(4),
        cost_estimate=cost(0, 0),
        name="route",
    )(held, one, two)


def pick_kernel(per, own, other, out_ref):
    out_ref[...] = jnp.where(on_own_side(per, 1), other[...], own[...])


def pick(own, other, per):
    return pl.pallas_call(
        functools.partial(pick_kernel, per),
        out_shape=in_vmem(own.shape),
        in_specs=[VMEM] * 2,
        out_specs=VMEM,
        compiler_params=grant(4),
        cost_estimate=cost(0, 0),
        name="pick",
    )(own, other)


def shift_of(left, inner):
    tags = left[left.shape[0] - TILE :, :MR].astype(jnp.float32)
    row = lax.broadcasted_iota(jnp.int32, tags.shape, 0)
    return jnp.max(jnp.where(row == inner, tags, -1.0)).astype(jnp.int32)


def pack_kernel(shift, left, right, packed, kept, shift_ref, sems):
    rows = left.shape[0]
    copies = [
        pltpu.make_async_copy(shift, shift_ref, sems.at[0]),
        pltpu.make_async_copy(left, packed.at[pl.ds(0, rows)], sems.at[1]),
        pltpu.make_async_copy(right, kept, sems.at[2]),
    ]
    for copy in copies:
        copy.start()
    copies[0].wait()
    row = lax.broadcasted_iota(jnp.int32, (TILE, ML), 0)
    tags = jnp.zeros((TILE, ML), jnp.float32)
    for inner in range(rows // ML):
        tags = jnp.where(row == inner, shift_ref[inner].astype(jnp.float32), tags)
    packed[rows:] = tags.astype(jnp.bfloat16)
    for copy in copies[1:]:
        copy.wait()


def pack(shift, left, right):
    return pl.pallas_call(
        pack_kernel,
        out_shape=[in_vmem((left.shape[0] + TILE, ML)), in_vmem(right.shape)],
        in_specs=[HBM] * 3,
        out_specs=[VMEM] * 2,
        scratch_shapes=[pltpu.SMEM(shift.shape, jnp.int32), pltpu.SemaphoreType.DMA((3,))],
        compiler_params=grant(8),
        cost_estimate=cost(0, 32 * 1024 * 1024),
        name="pack",
    )(in_hbm(shift), in_hbm(left), in_hbm(right))


def window_kernel(n_op, wave, window, sems):
    width = window.shape[2] - 2 * MR
    op = lax.axis_index("op")
    start = pl.multiple_of(op * width, MR)
    middle = pltpu.make_async_copy(
        wave.at[:, :, pl.ds(start, width)], window.at[:, :, pl.ds(MR, width)], sems.at[0]
    )
    middle.start()

    def edge(valid, source, target, sem):
        @pl.when(valid)
        def _():
            copy = pltpu.make_async_copy(
                wave.at[:, :, pl.ds(pl.multiple_of(source, MR), MR)], window.at[:, :, pl.ds(target, MR)], sem
            )
            copy.start()
            copy.wait()

        @pl.when(jnp.logical_not(valid))
        def _():
            window[:, :, pl.ds(target, MR)] = jnp.zeros((VECS, ML, MR), jnp.bfloat16)

    edge(op > 0, start - MR, 0, sems.at[1])
    edge(op < n_op - 1, start + width, MR + width, sems.at[2])
    middle.wait()


def window_of(wave, n_op):
    width = wave.shape[2] // n_op
    return pl.pallas_call(
        functools.partial(window_kernel, n_op),
        out_shape=in_vmem((VECS, ML, width + 2 * MR)),
        in_specs=[HBM],
        out_specs=VMEM,
        scratch_shapes=[pltpu.SemaphoreType.DMA((3,))],
        compiler_params=grant(4),
        cost_estimate=cost(0, 2 * 1024 * 1024),
        name="window",
    )(in_hbm(wave))


def left_kernel(*refs):
    *lefts, window, z_ref = refs
    per = z_ref.shape[0]
    width = per * MR
    terms = lefts[0].shape[0] // ML
    for piece, left in enumerate(lefts):
        for inner in range(terms):
            term = piece * terms + inner
            offset = pl.multiple_of((1 + shift_of(left, inner)) * MR, MR)
            for v in range(VECS):
                z = jnp.dot(
                    left[inner * ML : (inner + 1) * ML], window[v, :, pl.ds(offset, width)], preferred_element_type=jnp.float32
                ).astype(jnp.bfloat16)
                for column in range(per):
                    z_ref[column, v, :, term * MR : (term + 1) * MR] = z[:, column * MR : (column + 1) * MR]


def left_products(lefts, window):
    terms = len(lefts) * (lefts[0].shape[0] // ML)
    width = window.shape[2] - 2 * MR
    return pl.pallas_call(
        left_kernel,
        out_shape=in_vmem((width // MR, VECS, ML, terms * MR)),
        in_specs=[VMEM] * (len(lefts) + 1),
        out_specs=VMEM,
        compiler_params=grant(8 + 4 * width // MR),
        cost_estimate=cost(2 * terms * VECS * ML * ML * width, 1024 * 1024),
        name="left_products",
    )(*lefts, window)


def right_kernel(cls, per, z_ref, own, other, received, *refs):
    *lefts, zero_ref, low_ref, high_ref, total = refs
    sec = lax.axis_index("sec")
    column = (sec % per) ^ cls
    even = sec % 2 == 0
    settled = on_own_side(per, 1)
    half, terms = own.shape[0], own.shape[1]
    total[...] = jnp.zeros_like(total)
    for piece, left in enumerate(lefts):
        for inner in range(terms):
            term = piece * terms + inner
            kind = 1 + shift_of(left, inner)
            if piece < half:
                block = jnp.where(settled, own[piece, inner], other[piece, inner])
            else:
                block = received[piece - half, inner]
            for v in range(VECS):
                total[kind, v] += jnp.dot(
                    z_ref[column, v, :, term * MR : (term + 1) * MR], block, preferred_element_type=jnp.float32
                )
    for v in range(VECS):
        down, up = total[0, v], total[2, v]
        zero_ref[v] = total[1, v]
        low_ref[v] = jnp.where(even, up, down).astype(low_ref.dtype)
        high_ref[v] = jnp.where(even, down, up).astype(high_ref.dtype)


def right_products(cls, per, through, z, own, other, received, lefts):
    block = (VECS, ML, MR)
    low_type = jnp.float32 if through else jnp.bfloat16
    return pl.pallas_call(
        functools.partial(right_kernel, cls, per),
        out_shape=[jax.ShapeDtypeStruct(block, dtype) for dtype in (jnp.float32, low_type, jnp.bfloat16)],
        in_specs=[VMEM] * (4 + len(lefts)),
        out_specs=[VMEM] * 3,
        scratch_shapes=[in_vmem((3,) + block, jnp.float32)],
        compiler_params=grant(8),
        cost_estimate=cost(0, 0),
        name="right_products",
    )(z, own, other, received, *lefts)


def joined_kernel(low, passing, out_ref):
    out_ref[...] = (low[...] + passing[...].astype(jnp.float32)).astype(jnp.bfloat16)


def joined(low, passing):
    return pl.pallas_call(
        joined_kernel,
        out_shape=jax.ShapeDtypeStruct(low.shape, jnp.bfloat16),
        in_specs=[VMEM] * 2,
        out_specs=VMEM,
        compiler_params=grant(8),
        cost_estimate=cost(0, 0),
        name="joined",
    )(low, passing)


def early_kernel(per, through, *refs):
    parts, outs = refs[: len(refs) - per], refs[len(refs) - per :]
    direct = [cls for cls in range(per) if cls not in through]
    zeros, lows, highs = parts[:per], dict(zip(direct, parts[per:])), dict(zip(direct, parts[per + len(direct) :]))
    sec = lax.axis_index("sec")
    beyond = (sec ^ ((((sec + 1) ^ 1) + per - 1) % per)) % per

    def add(high):
        @pl.when(beyond == high)
        def _():
            for cls in range(per):
                for v in range(VECS):
                    total = zeros[cls][v].astype(jnp.float32)
                    if cls ^ 1 in lows:
                        total = total + lows[cls ^ 1][v].astype(jnp.float32)
                    if cls ^ high in highs:
                        total = total + highs[cls ^ high][v].astype(jnp.float32)
                    outs[cls][v] = total.astype(outs[cls].dtype)

    carry = 1
    while carry < per:
        add(carry)
        carry = 2 * carry + 1


def early_sums(per, through, parts):
    block = (VECS, ML, MR)
    return pl.pallas_call(
        functools.partial(early_kernel, per, through),
        out_shape=[in_vmem(block, jnp.float32 if cls ^ 1 in through else jnp.bfloat16) for cls in range(per)],
        in_specs=[VMEM] * len(parts),
        out_specs=[VMEM] * per,
        compiler_params=grant(8),
        cost_estimate=cost(0, 0),
        name="early_sums",
    )(*parts)


def sum_kernel(per, through, *refs):
    sums, lows = refs[:per], dict(zip(through, refs[per:]))
    out_hbm, late, sems = refs[per + len(through) :]
    sec = lax.axis_index("sec")
    copies = []
    for cls in sorted(range(per), key=lambda c: c ^ 1 in lows):
        column = pl.multiple_of(((sec % per) ^ cls) * MR, MR)
        source = sums[cls]
        if cls ^ 1 in lows:
            source = late.at[cls]
            late[cls] = (sums[cls][...] + lows[cls ^ 1][...].astype(jnp.float32)).astype(jnp.bfloat16)
        copies.append(pltpu.make_async_copy(source, out_hbm.at[:, :, pl.ds(column, MR)], sems.at[cls]))
        copies[-1].start()
    for copy in copies:
        copy.wait()


def summed(per, through, sums, lows):
    return pl.pallas_call(
        functools.partial(sum_kernel, per, through),
        out_shape=jax.ShapeDtypeStruct((VECS, ML, per * MR), jnp.bfloat16),
        in_specs=[VMEM] * (len(sums) + len(lows)),
        out_specs=HBM,
        scratch_shapes=[in_vmem((per, VECS, ML, MR)), pltpu.SemaphoreType.DMA((per,))],
        compiler_params=grant(8),
        name="summed",
    )(*sums, *lows)


def on_device(n_op, n_sec, wavefunction, left_ops, right_ops, term_shift):
    per = n_sec // n_op
    tie = lax.optimization_barrier
    matching = lax.axis_index("op") ^ (lax.axis_index("sec") // per)
    held = right_ops.reshape((1,) + right_ops.shape[:1] + right_ops.shape[2:])
    packed, kept = pack(term_shift, left_ops.transpose(1, 0, 2).reshape(-1, ML), held)
    window = window_of(wavefunction.transpose(1, 0, 2), n_op)
    lefts = [packed]
    bit = n_op // 2
    while bit > 1:
        one, two, window = tie((*towards_owner(held, n_op, n_sec, bit), window))
        same = (matching & bit) == 0
        held = kept = jnp.concatenate([jnp.where(same, kept, one), jnp.where(same, one, two)])
        lefts = lefts + [over_op(x, n_op, bit) for x in lefts]
        bit //= 2
    lefts = lefts + [over_op(x, n_op, 1) for x in lefts]
    owns = [held]
    bit = 1
    while bit < per:
        owns = owns + [over_sec(c, n_sec, bit) for c in owns]
        bit *= 2
    other, owns[1:] = tie((over_sec(owns[0], n_sec, per), owns[1:]))
    z = left_products(lefts, window)
    low = [(d, d ^ 1) for d in range(n_sec)]
    high = [(d, ((d + 1) ^ 1) - 1) for d in range(1, n_sec - 1)]
    turn = 2 % per
    through = sorted({0, turn}) if per <= 4 else []
    lows = []
    along = [(d, d + 2 if d % 2 else d - 2) for d in range(1, n_sec - 1)]
    settled = (matching & 1) == 0
    parts, others = [], [other]
    for cls, own in enumerate(owns):
        received = over_op(jnp.where(settled, other, own), n_op, 1)
        later = None
        if cls + 1 < per:
            half = own.shape[0] // 2
            step = (cls + 1) & -(cls + 1)
            later = [
                over_sec(owns[cls + 1][:half], n_sec, per),
                over_sec(others[(cls + 1) ^ step][half:], n_sec, step),
            ]
        zero, to_low, to_high = right_products(cls, per, cls in through, z, own, other, received, lefts)
        if cls in through:
            passing = lax.ppermute(to_high, "sec", along)
            parts += [zero, to_low, passing]
        else:
            parts += [zero, lax.ppermute(to_low, "sec", low), lax.ppermute(to_high, "sec", high)]
        if later is not None:
            later, parts[-3] = tie((later, zero.astype(jnp.bfloat16)))
            other = jnp.concatenate(later)
            others.append(other)
    for cls in through:
        own_low = tie((parts[3 * cls + 1], parts[3]))[0]
        lows.append(lax.ppermute(joined(own_low, parts[3 * (cls ^ turn) + 2]), "sec", low))
    direct = [cls for cls in range(per) if cls not in through]
    parts = parts[::3] + [parts[3 * cls + 1] for cls in direct] + [parts[3 * cls + 2] for cls in direct]
    sums = early_sums(per, through, parts)
    return summed(per, through, sums, lows).transpose(1, 0, 2)


def solution(mesh):
    in_specs = (P("sec", None, None), P("sec", "op", None), P("op", "sec", None, None), P("op"))
    out_specs = P("sec", None, "op")
    return jax.shard_map(
        functools.partial(on_device, mesh.shape["op"], mesh.shape["sec"]),
        mesh=mesh,
        in_specs=in_specs,
        out_specs=out_specs,
        check_vma=False,
    )
```

```python
import functools

import jax
import jax.numpy as jnp
from jax import lax
from jax.experimental import pallas as pl
from jax.experimental.pallas import tpu as pltpu
from jax.sharding import PartitionSpec as P

ML = 256
MR = 128
VECS = 3
TILE = 16
VMEM = pl.BlockSpec(memory_space=pltpu.VMEM)
HBM = pl.BlockSpec(memory_space=pltpu.HBM)


def in_vmem(shape, dtype=jnp.bfloat16):
    return pltpu.VMEM(shape, dtype)


def in_hbm(x):
    return pltpu.with_memory_space_constraint(x, pltpu.HBM)


def grant(mebibytes):
    return pltpu.CompilerParams(vmem_limit_bytes=mebibytes * 1024 * 1024)


def cost(flops, bytes_accessed):
    return pl.CostEstimate(flops=flops, bytes_accessed=bytes_accessed, transcendentals=0)


def over_op(x, n_op, bit):
    return lax.ppermute(x, "op", [(o, o ^ bit) for o in range(n_op)])


def over_sec(x, n_sec, bit):
    return lax.ppermute(x, "sec", [(d, d ^ bit) for d in range(n_sec)])


def on_own_side(per, bit):
    return ((lax.axis_index("op") ^ (lax.axis_index("sec") // per)) & bit) == 0


def towards_owner(held, n_op, n_sec, bit):
    per = n_sec // n_op
    first, second = [], []
    for o in range(n_op):
        for d in range(n_sec):
            source = o * n_sec + d
            far = d ^ (bit * per)
            if (o & bit) == ((d // per) & bit):
                first.append((source, o * n_sec + far))
            else:
                first.append((source, (o ^ bit) * n_sec + d))
                second.append((source, (o ^ bit) * n_sec + far))
    return lax.ppermute(held, ("op", "sec"), first), lax.ppermute(held, ("op", "sec"), second)


def route_kernel(per, bit, held, one, two, out_ref):
    half = held.shape[0]
    own = on_own_side(per, bit)
    out_ref[:half] = jnp.where(own, held[...], one[...])
    out_ref[half:] = jnp.where(own, one[...], two[...])


def route(held, one, two, per, bit):
    return pl.pallas_call(
        functools.partial(route_kernel, per, bit),
        out_shape=in_vmem((2 * held.shape[0],) + held.shape[1:]),
        in_specs=[VMEM] * 3,
        out_specs=VMEM,
        compiler_params=grant(4),
        cost_estimate=cost(0, 0),
        name="route",
    )(held, one, two)


def pick_kernel(per, own, other, out_ref):
    out_ref[...] = jnp.where(on_own_side(per, 1), other[...], own[...])


def pick(own, other, per):
    return pl.pallas_call(
        functools.partial(pick_kernel, per),
        out_shape=in_vmem(own.shape),
        in_specs=[VMEM] * 2,
        out_specs=VMEM,
        compiler_params=grant(4),
        cost_estimate=cost(0, 0),
        name="pick",
    )(own, other)


def shift_of(left, inner):
    tags = left[left.shape[0] - TILE :, :MR].astype(jnp.float32)
    row = lax.broadcasted_iota(jnp.int32, tags.shape, 0)
    return jnp.max(jnp.where(row == inner, tags, -1.0)).astype(jnp.int32)


def pack_kernel(shift, left, right, packed, kept, shift_ref, sems):
    rows = left.shape[0]
    copies = [
        pltpu.make_async_copy(shift, shift_ref, sems.at[0]),
        pltpu.make_async_copy(left, packed.at[pl.ds(0, rows)], sems.at[1]),
        pltpu.make_async_copy(right, kept, sems.at[2]),
    ]
    for copy in copies:
        copy.start()
    copies[0].wait()
    row = lax.broadcasted_iota(jnp.int32, (TILE, ML), 0)
    tags = jnp.zeros((TILE, ML), jnp.float32)
    for inner in range(rows // ML):
        tags = jnp.where(row == inner, shift_ref[inner].astype(jnp.float32), tags)
    packed[rows:] = tags.astype(jnp.bfloat16)
    for copy in copies[1:]:
        copy.wait()


def pack(shift, left, right):
    return pl.pallas_call(
        pack_kernel,
        out_shape=[in_vmem((left.shape[0] + TILE, ML)), in_vmem(right.shape)],
        in_specs=[HBM] * 3,
        out_specs=[VMEM] * 2,
        scratch_shapes=[pltpu.SMEM(shift.shape, jnp.int32), pltpu.SemaphoreType.DMA((3,))],
        compiler_params=grant(8),
        cost_estimate=cost(0, 32 * 1024 * 1024),
        name="pack",
    )(in_hbm(shift), in_hbm(left), in_hbm(right))


def window_kernel(n_op, wave, window, sems):
    width = window.shape[2] - 2 * MR
    op = lax.axis_index("op")
    start = pl.multiple_of(op * width, MR)
    middle = pltpu.make_async_copy(
        wave.at[:, :, pl.ds(start, width)], window.at[:, :, pl.ds(MR, width)], sems.at[0]
    )
    middle.start()

    def edge(valid, source, target, sem):
        @pl.when(valid)
        def _():
            copy = pltpu.make_async_copy(
                wave.at[:, :, pl.ds(pl.multiple_of(source, MR), MR)], window.at[:, :, pl.ds(target, MR)], sem
            )
            copy.start()
            copy.wait()

        @pl.when(jnp.logical_not(valid))
        def _():
            window[:, :, pl.ds(target, MR)] = jnp.zeros((VECS, ML, MR), jnp.bfloat16)

    edge(op > 0, start - MR, 0, sems.at[1])
    edge(op < n_op - 1, start + width, MR + width, sems.at[2])
    middle.wait()


def window_of(wave, n_op):
    width = wave.shape[2] // n_op
    return pl.pallas_call(
        functools.partial(window_kernel, n_op),
        out_shape=in_vmem((VECS, ML, width + 2 * MR)),
        in_specs=[HBM],
        out_specs=VMEM,
        scratch_shapes=[pltpu.SemaphoreType.DMA((3,))],
        compiler_params=grant(4),
        cost_estimate=cost(0, 2 * 1024 * 1024),
        name="window",
    )(in_hbm(wave))


def left_kernel(*refs):
    *lefts, window, z_ref = refs
    per = z_ref.shape[0]
    width = per * MR
    terms = lefts[0].shape[0] // ML
    for piece, left in enumerate(lefts):
        for inner in range(terms):
            term = piece * terms + inner
            offset = pl.multiple_of((1 + shift_of(left, inner)) * MR, MR)
            for v in range(VECS):
                z = jnp.dot(
                    left[inner * ML : (inner + 1) * ML], window[v, :, pl.ds(offset, width)], preferred_element_type=jnp.float32
                ).astype(jnp.bfloat16)
                for column in range(per):
                    z_ref[column, v, :, term * MR : (term + 1) * MR] = z[:, column * MR : (column + 1) * MR]


def left_products(lefts, window):
    terms = len(lefts) * (lefts[0].shape[0] // ML)
    width = window.shape[2] - 2 * MR
    return pl.pallas_call(
        left_kernel,
        out_shape=in_vmem((width // MR, VECS, ML, terms * MR)),
        in_specs=[VMEM] * (len(lefts) + 1),
        out_specs=VMEM,
        compiler_params=grant(8 + 4 * width // MR),
        cost_estimate=cost(2 * terms * VECS * ML * ML * width, 1024 * 1024),
        name="left_products",
    )(*lefts, window)


def right_kernel(cls, per, z_ref, own, other, received, *refs):
    *lefts, zero_ref, low_ref, high_ref, total = refs
    sec = lax.axis_index("sec")
    column = (sec % per) ^ cls
    even = sec % 2 == 0
    settled = on_own_side(per, 1)
    half, terms = own.shape[0], own.shape[1]
    total[...] = jnp.zeros_like(total)
    for piece, left in enumerate(lefts):
        for inner in range(terms):
            term = piece * terms + inner
            kind = 1 + shift_of(left, inner)
            if piece < half:
                block = jnp.where(settled, own[piece, inner], other[piece, inner])
            else:
                block = received[piece - half, inner]
            for v in range(VECS):
                total[kind, v] += jnp.dot(
                    z_ref[column, v, :, term * MR : (term + 1) * MR], block, preferred_element_type=jnp.float32
                )
    for v in range(VECS):
        down, up = total[0, v], total[2, v]
        zero_ref[v] = total[1, v]
        low_ref[v] = jnp.where(even, up, down).astype(low_ref.dtype)
        high_ref[v] = jnp.where(even, down, up).astype(high_ref.dtype)


def right_products(cls, per, through, z, own, other, received, lefts):
    block = (VECS, ML, MR)
    low_type = jnp.float32 if through else jnp.bfloat16
    return pl.pallas_call(
        functools.partial(right_kernel, cls, per),
        out_shape=[jax.ShapeDtypeStruct(block, dtype) for dtype in (jnp.float32, low_type, jnp.bfloat16)],
        in_specs=[VMEM] * (4 + len(lefts)),
        out_specs=[VMEM] * 3,
        scratch_shapes=[in_vmem((3,) + block, jnp.float32)],
        compiler_params=grant(8),
        cost_estimate=cost(0, 0),
        name="right_products",
    )(z, own, other, received, *lefts)


def joined_kernel(low, passing, out_ref):
    out_ref[...] = (low[...] + passing[...].astype(jnp.float32)).astype(jnp.bfloat16)


def joined(low, passing):
    return pl.pallas_call(
        joined_kernel,
        out_shape=jax.ShapeDtypeStruct(low.shape, jnp.bfloat16),
        in_specs=[VMEM] * 2,
        out_specs=VMEM,
        compiler_params=grant(8),
        cost_estimate=cost(0, 0),
        name="joined",
    )(low, passing)


def sum_kernel(per, direct, *refs):
    *parts, out_hbm, out_ref, sems = refs
    zeros, lows, highs = parts[:per], parts[per : 2 * per], dict(zip(direct, parts[2 * per :]))
    sec = lax.axis_index("sec")
    beyond = (sec ^ ((((sec + 1) ^ 1) + per - 1) % per)) % per
    copies = [pltpu.make_async_copy(out_ref.at[v], out_hbm.at[v], sems.at[v]) for v in range(VECS)]

    def add(high):
        @pl.when(beyond == high)
        def _():
            for v in range(VECS):
                for cls in range(per):
                    column = pl.multiple_of(((sec % per) ^ cls) * MR, MR)
                    total = zeros[cls][v].astype(jnp.float32) + lows[cls ^ 1][v].astype(jnp.float32)
                    if cls ^ high in highs:
                        total = total + highs[cls ^ high][v].astype(jnp.float32)
                    out_ref[v, :, pl.ds(column, MR)] = total.astype(jnp.bfloat16)
                copies[v].start()
            for copy in copies:
                copy.wait()

    carry = 1
    while carry < per:
        add(carry)
        carry = 2 * carry + 1


def summed(per, direct, parts):
    shape = (VECS, ML, per * MR)
    return pl.pallas_call(
        functools.partial(sum_kernel, per, direct),
        out_shape=jax.ShapeDtypeStruct(shape, jnp.bfloat16),
        in_specs=[VMEM] * len(parts),
        out_specs=HBM,
        scratch_shapes=[in_vmem(shape), pltpu.SemaphoreType.DMA((VECS,))],
        compiler_params=grant(8),
        name="summed",
    )(*parts)


def on_device(n_op, n_sec, wavefunction, left_ops, right_ops, term_shift):
    per = n_sec // n_op
    tie = lax.optimization_barrier
    matching = lax.axis_index("op") ^ (lax.axis_index("sec") // per)
    held = right_ops.reshape((1,) + right_ops.shape[:1] + right_ops.shape[2:])
    packed, kept = pack(term_shift, left_ops.transpose(1, 0, 2).reshape(-1, ML), held)
    window = window_of(wavefunction.transpose(1, 0, 2), n_op)
    lefts = [packed]
    bit = n_op // 2
    while bit > 1:
        one, two, window = tie((*towards_owner(held, n_op, n_sec, bit), window))
        same = (matching & bit) == 0
        held = kept = jnp.concatenate([jnp.where(same, kept, one), jnp.where(same, one, two)])
        lefts = lefts + [over_op(x, n_op, bit) for x in lefts]
        bit //= 2
    lefts = lefts + [over_op(x, n_op, 1) for x in lefts]
    owns = [held]
    bit = 1
    while bit < per:
        owns = owns + [over_sec(c, n_sec, bit) for c in owns]
        bit *= 2
    other, owns[1:] = tie((over_sec(owns[0], n_sec, per), owns[1:]))
    z = left_products(lefts, window)
    low = [(d, d ^ 1) for d in range(n_sec)]
    high = [(d, ((d + 1) ^ 1) - 1) for d in range(1, n_sec - 1)]
    turn = 2 % per
    through = sorted({0, turn}) if per <= 4 else []
    lows = []
    along = [(d, d + 2 if d % 2 else d - 2) for d in range(1, n_sec - 1)]
    settled = (matching & 1) == 0
    parts, others = [], [other]
    for cls, own in enumerate(owns):
        received = over_op(jnp.where(settled, other, own), n_op, 1)
        later = None
        if cls + 1 < per:
            half = own.shape[0] // 2
            step = (cls + 1) & -(cls + 1)
            later = [
                over_sec(owns[cls + 1][:half], n_sec, per),
                over_sec(others[(cls + 1) ^ step][half:], n_sec, step),
            ]
        zero, to_low, to_high = right_products(cls, per, cls in through, z, own, other, received, lefts)
        if cls in through:
            passing = lax.ppermute(to_high, "sec", along)
            parts += [zero, to_low, passing]
        else:
            parts += [zero, lax.ppermute(to_low, "sec", low), lax.ppermute(to_high, "sec", high)]
        if later is not None:
            later, parts[-3] = tie((later, zero.astype(jnp.bfloat16)))
            other = jnp.concatenate(later)
            others.append(other)
    for cls in through:
        own_low = tie((parts[3 * cls + 1], parts[3]))[0]
        lows.append(lax.ppermute(joined(own_low, parts[3 * (cls ^ turn) + 2]), "sec", low))
    for cls, part in zip(through, lows):
        parts[3 * cls + 1] = part
    direct = [cls for cls in range(per) if cls not in through]
    parts = parts[::3] + parts[1::3] + [parts[3 * cls + 2] for cls in direct]
    return summed(per, direct, parts).transpose(1, 0, 2)


def solution(mesh):
    in_specs = (P("sec", None, None), P("sec", "op", None), P("op", "sec", None, None), P("op"))
    out_specs = P("sec", None, "op")
    return jax.shard_map(
        functools.partial(on_device, mesh.shape["op"], mesh.shape["sec"]),
        mesh=mesh,
        in_specs=in_specs,
        out_specs=out_specs,
        check_vma=False,
    )
```
